128 devices in a mesh: shard: 16 (over z, x), rep: 8 (over y, core).
Axes of the slice: x: 4, y: 4, z: 4, core: 2. Of those that a mesh axis runs over, the one named last changes fastest.
Arguments:
- embeddings: bfloat16 [256, 512, 768], P('shard'), may hold values from -8.375 to 8.375
- labels: bfloat16 [256, 1000, 512], P('shard', 'rep'), may hold values from -30 to 30
- block_pairs: int32 [640, 2], replicated, may hold values from 0 to 255, as said below
- block_slot: int32 [256], replicated, may hold values from 0 to 255, as said below
Outputs:
- propagated: float32 [256, 1000, 512], P('shard', 'rep')
The draws below stay inside these ranges and needn't reach their ends.
Inputs may be any that keep to these rules, and one draw needn't show every extreme that they name: `block_slot`: blocks 16 * g to 16 * g + 15 form cluster g; they lie in the slots o * 16 + g, one for each o in 0 to 15, in an order drawn from the seed. Every slot is used once. `block_pairs`: rows 40 * g to 40 * g + 39 join two different blocks of cluster g, the first number smaller; no pair appears twice; every block is in some pair.
All inputs are finite; a program needn't handle non-finite values.
Results may differ from the reference program's by a relative error of at most 0.0065.
Values may be sent and summed in bfloat16 or wider, within the bound.
A program may use at most 256 MiB of HBM per device.

```python
import math
import jax
import jax.numpy as jnp
import numpy as np
from jax import lax

D = 768
C = 1000
BR = 512
ITERS = 2
CLUSTER = 16
NB = 256
CPAIRS = 40
NPAIRS = 640
N_SHARD = 16


def draw_block_pairs(key, part):
    upper = np.triu_indices(CLUSTER, 1)
    first_cand = jnp.asarray(upper[0].astype(np.int32))
    second_cand = jnp.asarray(upper[1].astype(np.int32))
    candidates = first_cand.shape[0]

    def one_cluster(cluster_key):
        order_key, rank_key = jax.random.split(cluster_key)
        order = jax.random.permutation(order_key, CLUSTER)
        position = jnp.argsort(order, stable=True).astype(jnp.int32)
        chain = (jnp.abs(position[first_cand] - position[second_cand]) == 1).astype(jnp.int32)
        ranking = jax.random.permutation(rank_key, candidates).astype(jnp.int32)
        score = ranking + chain * candidates
        _, chosen = lax.top_k(score, CPAIRS)
        return (first_cand[chosen], second_cand[chosen])
    cluster_keys = jax.random.split(jax.random.fold_in(key, 17), N_SHARD)
    first_idx, second_idx = jax.vmap(one_cluster)(cluster_keys)
    offsets = (jnp.arange(N_SHARD, dtype=jnp.int32) * CLUSTER)[:, None]
    joined = jnp.stack([first_idx + offsets, second_idx + offsets], axis=-1)
    return joined.reshape(NPAIRS, 2).astype(jnp.int32)


def draw_block_slot(key, part):
    cluster_keys = jax.random.split(jax.random.fold_in(key, 29), N_SHARD)
    owners = jax.vmap(lambda cluster_key: jax.random.permutation(cluster_key, CLUSTER))(cluster_keys)
    slots = owners.astype(jnp.int32) * N_SHARD + jnp.arange(N_SHARD, dtype=jnp.int32)[:, None]
    return slots.reshape(NB).astype(jnp.int32)


def level_of(stream_key, extent, shards, low, high):
    def one(dim, parts):
        heights = jax.random.uniform(jax.random.fold_in(jax.random.fold_in(stream_key, 6), dim), (parts,), jnp.float32, low / len(shards), high / len(shards))
        return jnp.repeat(jnp.exp(heights), extent[dim] // parts).reshape((-1,) + (1,) * (len(extent) - dim - 1))

    loudness = one(*shards[0])
    for cut in shards[1:]:
        loudness = loudness * one(*cut)
    return loudness


def scatter_about(rng, shape, deviation, reach, cuts=(), kind=jnp.bfloat16):
    factor_of = level_of(rng, shape, cuts, -0.22, 0.18) if cuts else 1.0
    entries = jax.random.normal(rng, shape, jnp.float32) * deviation * factor_of
    return jnp.minimum(jnp.maximum(entries, -reach), reach).astype(kind)


def setup_inputs(seed: int = 0) -> dict:
    streams_of = jax.random.split(jax.random.key(seed), 5)
    return {
        "embeddings": scatter_about(streams_of[0], (NB, BR, D), 1.4, 8.375, ((0, 16),)),
        "labels": scatter_about(streams_of[1], (NB, C, BR), 5.0, 30.0, ((0, 16), (1, 8))),
        "block_pairs": draw_block_pairs(jax.random.fold_in(streams_of[4], 71), 0),
        "block_slot": draw_block_slot(jax.random.fold_in(streams_of[4], 71), 0),
    }


ALPHA = 0.9

def reference(embeddings, labels, block_pairs, block_slot):
    kernel_scale = 1.0 / math.sqrt(embeddings.shape[2])
    slot_a = jnp.take(block_slot, block_pairs[:, 0]).astype(jnp.int32)
    slot_b = jnp.take(block_slot, block_pairs[:, 1]).astype(jnp.int32)

    def kernel_tile(first_slot, second_slot):
        scores = jnp.dot(embeddings[first_slot], embeddings[second_slot].T, preferred_element_type=jnp.float32)
        return jnp.exp(scores * kernel_scale)

    def add_degree(degree, slot_pair):
        first_slot, second_slot = slot_pair
        kernel = kernel_tile(first_slot, second_slot)
        degree = degree.at[first_slot].add(lax.optimization_barrier(jnp.sum(kernel, axis=1)))
        degree = degree.at[second_slot].add(lax.optimization_barrier(jnp.sum(kernel, axis=0)))
        return (degree, None)
    degree, _ = lax.scan(add_degree, jnp.zeros((NB, BR), jnp.float32), (slot_a, slot_b))
    scaling = (1.0 / jnp.sqrt(degree))[:, None, :]
    seed_labels = labels.astype(jnp.float32)
    label_field = seed_labels
    for iteration in range(ITERS):
        outgoing = (label_field * scaling).astype(jnp.bfloat16)

        def add_products(running, slot_pair):
            first_slot, second_slot = slot_pair
            kernel_bf = kernel_tile(first_slot, second_slot).astype(jnp.bfloat16)
            running = running.at[first_slot].add(jnp.dot(outgoing[second_slot], kernel_bf.T, preferred_element_type=jnp.float32))
            running = running.at[second_slot].add(jnp.dot(outgoing[first_slot], kernel_bf, preferred_element_type=jnp.float32))
            return (running, None)
        products, _ = lax.scan(add_products, jnp.zeros(labels.shape, jnp.float32), (slot_a, slot_b))
        label_field = ALPHA * scaling * products + (1.0 - ALPHA) * seed_labels
    return label_field
```

```python
import functools
import math

import jax
import jax.numpy as jnp
from jax import lax
from jax.experimental import pallas as pl
from jax.experimental.pallas import tpu as pltpu
from jax.sharding import PartitionSpec as P

ITERS = 2
ALPHA = 0.9

SLOTS = 16
SIDE = 4
PAIRS = 40
ROWS = 512
DIM = 768
CLASSES = 125
PAD = 128
HALF = ROWS // 2
LANES = 128
UNROLL = 4

MESH = pl.DeviceIdType.MESH
NT = (((1,), (1,)), ((), ()))
NN = (((1,), (0,)), ((), ()))
BF = jnp.bfloat16
F32 = jnp.float32


def dot(a, b, dims):
    return lax.dot_general(a, b, dims, preferred_element_type=F32)


def index_table(block_pairs, block_slot):
    group = lax.axis_index("shard")
    pairs = lax.dynamic_slice_in_dim(block_pairs, group * PAIRS, PAIRS, 0)
    slots = lax.dynamic_slice_in_dim(block_slot, group * SLOTS, SLOTS, 0)
    local = (pairs - group * SLOTS).reshape(-1)
    members = jnp.arange(SLOTS, dtype=jnp.int32)
    dest = jnp.sum(jnp.where(local[:, None] == members[None, :], (slots // SLOTS)[None, :], 0), axis=1)
    term = jnp.arange(2 * PAIRS, dtype=jnp.int32)
    before = (dest[:, None] == dest[None, :]) & (term[None, :] < term[:, None])
    prev = jnp.max(jnp.where(before, term[None, :], -1), axis=1)
    prev = jnp.where(prev < 0, 2 * PAIRS, prev)
    last = jnp.max(jnp.where(dest[None, :] == members[:, None], term[None, :], 0), axis=1)
    return jnp.concatenate([dest, prev, last]).astype(jnp.int32)


def main_kernel(
    idx, emb, lab, ret,
    E, K, T, W, LT, SB, L, O, O2, R, SC,
    se, re, sy, ry, sd, rd, sl, rl, sr, rr, loc,
):
    me = lax.axis_index("shard")
    rep = lax.axis_index("rep")
    y, core = rep // 2, rep % 2
    z, x = me // SIDE, me % SIDE
    up = ((y + 1) % SIDE) * 2 + core
    down = ((y + SIDE - 1) % SIDE) * 2 + core
    sibling = y * 2 + (1 - core)
    quarters = (y, (y + 2) % SIDE, (y + 3) % SIDE, (y + 1) % SIDE)

    def dest_of(u):
        return idx[u]

    def prev_of(u):
        return idx[2 * PAIRS + u]

    def last_of(s):
        return idx[4 * PAIRS + s]

    def to(k):
        return ((z + k // SIDE) % SIDE) * SIDE + (x + k % SIDE) % SIDE

    def source(k):
        return ((z + SIDE - k // SIDE) % SIDE) * SIDE + (x + SIDE - k % SIDE) % SIDE

    def remote(src, dst, send, recv, shard, r):
        return pltpu.make_async_remote_copy(
            src, dst, send, recv, device_id={"shard": shard, "rep": r}, device_id_type=MESH
        )

    def emb_copy(k, i):
        q = quarters[i]
        return remote(emb.at[to(k), q, core], E.at[me, q, core], se.at[k, i], re.at[k, i], to(k), rep)

    def y_copy(k, i):
        piece = E.at[source(k), quarters[0], core]
        return remote(piece, piece, sy.at[k, i], ry.at[k, i], me, (up, down)[i])

    def sib_copy(k, i):
        piece = E.at[source(k), quarters[i], core]
        return remote(piece, piece, sd.at[k, i], rd.at[k, i], me, sibling)

    def lab_copy(k):
        return remote(SB.at[to(k)], L.at[me], sl.at[k], rl.at[k], to(k), rep)

    def ret_copy(k, h):
        cols = pl.ds(h * HALF, HALF)
        return remote(
            SB.at[to(k), :, cols], ret.at[me, :, cols], sr.at[k, h], rr.at[k, h], to(k), rep
        )

    def ret_own(h):
        cols = pl.ds(h * HALF, HALF)
        return pltpu.make_async_copy(SB.at[me, :, cols], ret.at[me, :, cols], loc.at[h])

    own_emb = pltpu.make_async_copy(emb.at[me], E.at[me], loc.at[0])
    own_lab = pltpu.make_async_copy(lab, LT, loc.at[1])
    own_emb.start()
    own_lab.start()

    barrier = pltpu.get_barrier_semaphore()

    @pl.loop(1, SLOTS)
    def _(k):
        pl.semaphore_signal(barrier, inc=1, device_id={"shard": to(k), "rep": rep}, device_id_type=MESH)

    for r in (up, down, sibling):
        pl.semaphore_signal(barrier, inc=1, device_id={"shard": me, "rep": r}, device_id_type=MESH)
    pl.semaphore_wait(barrier, SLOTS + 2)

    for i in range(2):
        @pl.loop(1, SLOTS)
        def _(k):
            emb_copy(k, i).start()

    T[2 * PAIRS] = jnp.zeros((PAD, HALF), F32)
    R[2 * PAIRS] = jnp.zeros((1, ROWS), F32)

    own_lab.wait()
    for c in range(ROWS // LANES):
        cols = slice(c * LANES, (c + 1) * LANES)
        b = c % 2
        W[b, 0 : SLOTS * CLASSES, :] = LT[:, cols].astype(F32)
        W[b, SLOTS * CLASSES : SLOTS * PAD, :] = jnp.zeros((SLOTS * (PAD - CLASSES), LANES), F32)
        for s in range(SLOTS):
            SB[s, :, cols] = W[b, pl.ds(s, PAD, stride=SLOTS), :].astype(BF)
    L[me] = SB[me]

    @pl.loop(1, SLOTS)
    def _(k):
        lab_copy(k).start()

    @pl.loop(1, SLOTS)
    def _(k):
        emb_copy(k, 0).wait_recv()
        y_copy(k, 0).start()
        y_copy(k, 1).start()
        sib_copy(k, 0).start()

    @pl.loop(1, SLOTS)
    def _(k):
        y_copy(k, 0).wait_recv()
        y_copy(k, 1).wait_recv()
        sib_copy(k, 2).start()
        sib_copy(k, 3).start()
        emb_copy(k, 1).wait_recv()
        sib_copy(k, 1).start()

    @pl.loop(1, SLOTS)
    def _(k):
        for i in range(4):
            sib_copy(k, i).wait_recv()
    own_emb.wait()

    scale = math.log2(math.e) / math.sqrt(DIM)

    def tile(t):
        a = E[dest_of(2 * t)].reshape(ROWS, DIM)
        b = E[dest_of(2 * t + 1)].reshape(ROWS, DIM)
        kernel = jnp.exp2(dot(a, b, NT) * scale)
        K[t] = kernel.astype(BF)
        cols = jnp.sum(kernel, axis=0, keepdims=True)
        part = kernel[:, 0:128] + kernel[:, 128:256] + kernel[:, 256:384] + kernel[:, 384:512]
        rows = jnp.sum(part.T, axis=0, keepdims=True)
        for u, sums in ((2 * t, rows), (2 * t + 1, cols)):
            R[u] = sums + R[prev_of(u)]

    @pl.loop(0, PAIRS // UNROLL)
    def _(i):
        for j in range(UNROLL):
            tile(i * UNROLL + j)

    @pl.loop(1, SLOTS)
    def _(k):
        lab_copy(k).wait()

    @pl.loop(0, SLOTS)
    def _(s):
        scaling = 1.0 / jnp.sqrt(R[last_of(s)])
        SC[s] = scaling
        O[s] = (L[s].astype(F32) * scaling).astype(BF)

    def products(src, h):
        cols = slice(h * HALF, (h + 1) * HALF)

        def pair(t):
            first, second = dest_of(2 * t), dest_of(2 * t + 1)
            to_first = dot(src[second], K[t, cols, :], NT)
            to_second = dot(src[first], K[t, :, cols], NN)
            for u, product in ((2 * t, to_first), (2 * t + 1, to_second)):
                T[u] = product + T[prev_of(u)]

        @pl.loop(0, PAIRS // UNROLL)
        def _(i):
            for j in range(UNROLL):
                pair(i * UNROLL + j)

    for h in range(2):
        cols = slice(h * HALF, (h + 1) * HALF)
        products(O, h)

        @pl.loop(0, SLOTS)
        def _(s):
            scaling = SC[s, :, cols]
            field = (ALPHA * scaling) * T[last_of(s)] + (1.0 - ALPHA) * L[s, :, cols].astype(F32)
            O2[s, :, cols] = (field * scaling).astype(BF)

    for h in range(2):
        cols = slice(h * HALF, (h + 1) * HALF)
        products(O2, h)

        def finish(s):
            SB[s, :, cols] = ((ALPHA * SC[s, :, cols]) * T[last_of(s)]).astype(BF)

        @pl.loop(1, SLOTS)
        def _(k):
            finish(to(k))
            ret_copy(k, h).start()

        finish(me)
        ret_own(h).start()

    @pl.loop(1, SLOTS)
    def _(k):
        for i in range(2):
            emb_copy(k, i).wait_send()
            y_copy(k, i).wait_send()
        for i in range(4):
            sib_copy(k, i).wait_send()

    for h in range(2):
        @pl.loop(1, SLOTS)
        def _(k):
            ret_copy(k, h).wait()
        ret_own(h).wait()


def finish_kernel(ret, lab, out, W):
    for c in range(ROWS // LANES):
        cols = slice(c * LANES, (c + 1) * LANES)
        for s in range(SLOTS):
            W[c, pl.ds(s, 16, stride=SLOTS), :] = ret[s, :, cols].astype(F32)
        out[:, cols] = W[c] + (1.0 - ALPHA) * lab[:, cols].astype(F32)


def body(embeddings, labels, block_pairs, block_slot):
    idx = index_table(block_pairs, block_slot)
    emb = embeddings.reshape(SLOTS, SIDE, 2, ROWS // (2 * SIDE), DIM)
    lab = jnp.transpose(labels, (1, 0, 2)).reshape(CLASSES * SLOTS, ROWS)
    sems = pltpu.SemaphoreType.DMA
    ret = pl.pallas_call(
        main_kernel,
        out_shape=jax.ShapeDtypeStruct((SLOTS, PAD, ROWS), BF),
        in_specs=[
            pl.BlockSpec(memory_space=pltpu.SMEM),
            pl.BlockSpec(memory_space=pl.ANY),
            pl.BlockSpec(memory_space=pl.ANY),
        ],
        out_specs=pl.BlockSpec(memory_space=pl.ANY),
        scratch_shapes=[
            pltpu.VMEM((SLOTS, SIDE, 2, ROWS // (2 * SIDE), DIM), BF),
            pltpu.VMEM((PAIRS, ROWS, ROWS), BF),
            pltpu.VMEM((2 * PAIRS + 1, PAD, HALF), F32),
            pltpu.VMEM((2, SLOTS * PAD, LANES), F32),
            pltpu.VMEM((SLOTS * CLASSES, ROWS), BF),
            pltpu.VMEM((SLOTS, PAD, ROWS), BF),
            pltpu.VMEM((SLOTS, PAD, ROWS), BF),
            pltpu.VMEM((SLOTS, PAD, ROWS), BF),
            pltpu.VMEM((SLOTS, PAD, ROWS), BF),
            pltpu.VMEM((2 * PAIRS + 1, 1, ROWS), F32),
            pltpu.VMEM((SLOTS, 1, ROWS), F32),
            sems((SLOTS, 2)), sems((SLOTS, 2)),
            sems((SLOTS, 2)), sems((SLOTS, 2)),
            sems((SLOTS, 4)), sems((SLOTS, 4)),
            sems((SLOTS,)), sems((SLOTS,)),
            sems((SLOTS, 2)), sems((SLOTS, 2)),
            sems((2,)),
        ],
        compiler_params=pltpu.CompilerParams(
            vmem_limit_bytes=61 * 2**20, collective_id=0, has_side_effects=True
        ),
    )(idx, emb, lab)
    block = 16 * SLOTS
    out = pl.pallas_call(
        finish_kernel,
        out_shape=jax.ShapeDtypeStruct((CLASSES * SLOTS, ROWS), F32),
        grid=(PAD // 16,),
        in_specs=[
            pl.BlockSpec((SLOTS, 16, ROWS), lambda i: (0, i, 0)),
            pl.BlockSpec((block, ROWS), lambda i: (i, 0)),
        ],
        out_specs=pl.BlockSpec((block, ROWS), lambda i: (i, 0)),
        scratch_shapes=[pltpu.VMEM((ROWS // LANES, block, LANES), F32)],
    )(ret, lab)
    return jnp.transpose(out.reshape(CLASSES, SLOTS, ROWS), (1, 0, 2))


def solution(mesh):
    return jax.shard_map(
        body,
        mesh=mesh,
        in_specs=(P("shard", None, None), P("shard", "rep", None), P(), P()),
        out_specs=P("shard", "rep", None),
        check_vma=False,
    )
```

```python
import functools
import math

import jax
import jax.numpy as jnp
from jax import lax
from jax.experimental import pallas as pl
from jax.experimental.pallas import tpu as pltpu
from jax.sharding import PartitionSpec as P

ITERS = 2
ALPHA = 0.9

SLOTS = 16
SIDE = 4
PAIRS = 40
ROWS = 512
DIM = 768
CLASSES = 125
PAD = 128
HALF = ROWS // 2
LANES = 128
UNROLL = 4
LEAD = 13

MESH = pl.DeviceIdType.MESH
NT = (((1,), (1,)), ((), ()))
NN = (((1,), (0,)), ((), ()))
BF = jnp.bfloat16
F32 = jnp.float32


def dot(a, b, dims):
    return lax.dot_general(a, b, dims, preferred_element_type=F32)


def main_kernel(
    pairs, slots, emb, lab, out,
    E, K, T, W, LT, SB, L, O, O2, R, SC, idx,
    se, re, sy, ry, sd, rd, sl, rl, sr, rr, so, loc,
):
    me = lax.axis_index("shard")
    rep = lax.axis_index("rep")
    y, core = rep // 2, rep % 2
    z, x = me // SIDE, me % SIDE
    up = ((y + 1) % SIDE) * 2 + core
    down = ((y + SIDE - 1) % SIDE) * 2 + core
    sibling = y * 2 + (1 - core)
    quarters = (y, (y + 2) % SIDE, (y + 3) % SIDE, (y + 1) % SIDE)

    def dest_of(u):
        return idx[u]

    def prev_of(u):
        return idx[2 * PAIRS + u]

    def last_of(s):
        return idx[4 * PAIRS + s]

    def to(k):
        return ((z + k // SIDE) % SIDE) * SIDE + (x + k % SIDE) % SIDE

    def source(k):
        return ((z + SIDE - k // SIDE) % SIDE) * SIDE + (x + SIDE - k % SIDE) % SIDE

    def remote(src, dst, send, recv, shard, r):
        return pltpu.make_async_remote_copy(
            src, dst, send, recv, device_id={"shard": shard, "rep": r}, device_id_type=MESH
        )

    def landing(g):
        return LT.at[pl.ds(g * PAD, PAD), :]

    def emb_copy(k, i):
        q = quarters[i]
        return remote(emb.at[to(k), q, core], E.at[me, q, core], se.at[k, i], re.at[k, i], to(k), rep)

    def y_copy(k, i):
        piece = E.at[source(k), quarters[0], core]
        return remote(piece, piece, sy.at[k, i], ry.at[k, i], me, (up, down)[i])

    def sib_copy(k, i):
        piece = E.at[source(k), quarters[i], core]
        return remote(piece, piece, sd.at[k, i], rd.at[k, i], me, sibling)

    def lab_copy(k):
        return remote(SB.at[to(k)], L.at[me], sl.at[k], rl.at[k], to(k), rep)

    def ret_copy(k, h):
        cols = pl.ds(h * HALF, HALF)
        return remote(
            SB.at[to(k), :, cols], landing(me).at[:, cols], sr.at[k, h], rr.at[k, h], to(k), rep
        )

    def ret_own(h):
        cols = pl.ds(h * HALF, HALF)
        return pltpu.make_async_copy(SB.at[me, :, cols], landing(me).at[:, cols], loc.at[h])

    def out_copies(h):
        cols = pl.ds(h * HALF, HALF)
        full = SLOTS * CLASSES // PAD
        rest = SLOTS * CLASSES - full * PAD
        yield from (
            pltpu.make_async_copy(O.at[i, :, cols], out.at[pl.ds(i * PAD, PAD), cols], so.at[h, i])
            for i in range(full)
        )
        yield pltpu.make_async_copy(
            O.at[full, pl.ds(0, rest), cols], out.at[pl.ds(full * PAD, rest), cols], so.at[h, full]
        )

    own_emb = pltpu.make_async_copy(emb.at[me], E.at[me], loc.at[0])
    own_lab = pltpu.make_async_copy(lab, LT.at[pl.ds(0, SLOTS * CLASSES), :], loc.at[1])
    own_emb.start()
    own_lab.start()

    barrier = pltpu.get_barrier_semaphore()

    @pl.loop(1, SLOTS)
    def _(k):
        pl.semaphore_signal(barrier, inc=1, device_id={"shard": to(k), "rep": rep}, device_id_type=MESH)

    for r in (up, down, sibling):
        pl.semaphore_signal(barrier, inc=1, device_id={"shard": me, "rep": r}, device_id_type=MESH)
    pl.semaphore_wait(barrier, SLOTS + 2)

    @pl.loop(1, SLOTS)
    def _(k):
        emb_copy(k, 0).start()

    def walk(t, last):
        for end in range(2):
            u = 2 * t + end
            dest = slots[pairs[end, me * PAIRS + t]] // SLOTS
            idx[u] = dest
            prev = 2 * PAIRS
            for s in range(SLOTS):
                prev = jnp.where(dest == s, last[s], prev)
            idx[2 * PAIRS + u] = prev
            last = tuple(jnp.where(dest == s, u, last[s]) for s in range(SLOTS))
        return last

    last = lax.fori_loop(0, PAIRS, walk, (jnp.int32(2 * PAIRS),) * SLOTS)
    for s in range(SLOTS):
        idx[4 * PAIRS + s] = last[s]

    T[2 * PAIRS] = jnp.zeros((PAD, HALF), F32)
    R[2 * PAIRS] = jnp.zeros((1, ROWS), F32)

    @pl.loop(1, SLOTS)
    def _(k):
        emb_copy(k, 0).wait_recv()
        y_copy(k, 0).start()
        y_copy(k, 1).start()
        sib_copy(k, 0).start()
        emb_copy(k, 1).start()

    own_lab.wait()
    for c in range(ROWS // LANES):
        cols = slice(c * LANES, (c + 1) * LANES)
        b = c % 2
        W[b, 0 : SLOTS * CLASSES, :] = LT[0 : SLOTS * CLASSES, cols].astype(F32)
        W[b, SLOTS * CLASSES : SLOTS * PAD, :] = jnp.zeros((SLOTS * (PAD - CLASSES), LANES), F32)
        for s in range(SLOTS):
            SB[s, :, cols] = W[b, pl.ds(s, PAD, stride=SLOTS), :].astype(BF)
    L[me] = SB[me]

    def second_half(k):
        y_copy(k, 0).wait_recv()
        y_copy(k, 1).wait_recv()
        sib_copy(k, 2).start()
        sib_copy(k, 3).start()
        emb_copy(k, 1).wait_recv()
        sib_copy(k, 1).start()

    pl.loop(1, LEAD)(second_half)

    @pl.loop(1, SLOTS)
    def _(k):
        lab_copy(k).start()

    pl.loop(LEAD, SLOTS)(second_half)

    @pl.loop(1, SLOTS)
    def _(k):
        for i in range(4):
            sib_copy(k, i).wait_recv()
    own_emb.wait()

    scale = math.log2(math.e) / math.sqrt(DIM)

    def tile(t):
        a = E[dest_of(2 * t)].reshape(ROWS, DIM)
        b = E[dest_of(2 * t + 1)].reshape(ROWS, DIM)
        kernel = jnp.exp2(dot(a, b, NT) * scale)
        K[t] = kernel.astype(BF)
        cols = jnp.sum(kernel, axis=0, keepdims=True)
        part = kernel[:, 0:128] + kernel[:, 128:256] + kernel[:, 256:384] + kernel[:, 384:512]
        rows = jnp.sum(part.T, axis=0, keepdims=True)
        for u, sums in ((2 * t, rows), (2 * t + 1, cols)):
            R[u] = sums + R[prev_of(u)]

    @pl.loop(0, PAIRS // UNROLL)
    def _(i):
        for j in range(UNROLL):
            tile(i * UNROLL + j)

    @pl.loop(1, SLOTS)
    def _(k):
        lab_copy(k).wait()

    @pl.loop(0, SLOTS)
    def _(s):
        scaling = 1.0 / jnp.sqrt(R[last_of(s)])
        SC[s] = scaling
        O[s] = (L[s].astype(F32) * scaling).astype(BF)

    def products(src, h):
        cols = slice(h * HALF, (h + 1) * HALF)

        def pair(t):
            first, second = dest_of(2 * t), dest_of(2 * t + 1)
            to_first = dot(src[second], K[t, cols, :], NT)
            to_second = dot(src[first], K[t, :, cols], NN)
            for u, product in ((2 * t, to_first), (2 * t + 1, to_second)):
                T[u] = product + T[prev_of(u)]

        @pl.loop(0, PAIRS // UNROLL)
        def _(i):
            for j in range(UNROLL):
                pair(i * UNROLL + j)

    for h in range(2):
        cols = slice(h * HALF, (h + 1) * HALF)
        products(O, h)

        @pl.loop(0, SLOTS)
        def _(s):
            scaling = SC[s, :, cols]
            field = (ALPHA * scaling) * T[last_of(s)] + (1.0 - ALPHA) * L[s, :, cols].astype(F32)
            O2[s, :, cols] = (field * scaling).astype(BF)

    for h in range(2):
        cols = slice(h * HALF, (h + 1) * HALF)
        products(O2, h)

        def finish(s):
            SB[s, :, cols] = ((ALPHA * SC[s, :, cols]) * T[last_of(s)]).astype(BF)

        @pl.loop(1, SLOTS)
        def _(k):
            finish(to(k))
            ret_copy(k, h).start()

        finish(me)
        ret_own(h).start()

    @pl.loop(1, SLOTS)
    def _(k):
        for i in range(2):
            emb_copy(k, i).wait_send()
            y_copy(k, i).wait_send()
        for i in range(4):
            sib_copy(k, i).wait_send()

    for h in range(2):
        @pl.loop(1, SLOTS)
        def _(k):
            ret_copy(k, h).wait()

        ret_own(h).wait()
        for c in range(2):
            cols = slice(h * HALF + c * LANES, h * HALF + (c + 1) * LANES)
            for s in range(SLOTS):
                W[c, pl.ds(s, PAD, stride=SLOTS), :] = LT[s * PAD : (s + 1) * PAD, cols].astype(F32)
            for i in range(SLOTS):
                O[i, :, cols] = W[c, i * PAD : (i + 1) * PAD, :].astype(BF)
        for copy in out_copies(h):
            copy.start()

    for h in range(2):
        for copy in out_copies(h):
            copy.wait()


def body(embeddings, labels, block_pairs, block_slot):
    emb = embeddings.reshape(SLOTS, SIDE, 2, ROWS // (2 * SIDE), DIM)
    lab = jnp.transpose(labels, (1, 0, 2)).reshape(CLASSES * SLOTS, ROWS)
    sems = pltpu.SemaphoreType.DMA
    ret = pl.pallas_call(
        main_kernel,
        out_shape=jax.ShapeDtypeStruct((CLASSES * SLOTS, ROWS), BF),
        in_specs=[
            pl.BlockSpec(memory_space=pltpu.SMEM),
            pl.BlockSpec(memory_space=pltpu.SMEM),
            pl.BlockSpec(memory_space=pl.ANY),
            pl.BlockSpec(memory_space=pl.ANY),
        ],
        out_specs=pl.BlockSpec(memory_space=pl.ANY),
        scratch_shapes=[
            pltpu.VMEM((SLOTS, SIDE, 2, ROWS // (2 * SIDE), DIM), BF),
            pltpu.VMEM((PAIRS, ROWS, ROWS), BF),
            pltpu.VMEM((2 * PAIRS + 1, PAD, HALF), F32),
            pltpu.VMEM((2, SLOTS * PAD, LANES), F32),
            pltpu.VMEM((SLOTS * PAD, ROWS), BF),
            pltpu.VMEM((SLOTS, PAD, ROWS), BF),
            pltpu.VMEM((SLOTS, PAD, ROWS), BF),
            pltpu.VMEM((SLOTS, PAD, ROWS), BF),
            pltpu.VMEM((SLOTS, PAD, ROWS), BF),
            pltpu.VMEM((2 * PAIRS + 1, 1, ROWS), F32),
            pltpu.VMEM((SLOTS, 1, ROWS), F32),
            pltpu.SMEM((4 * PAIRS + SLOTS,), jnp.int32),
            sems((SLOTS, 2)), sems((SLOTS, 2)),
            sems((SLOTS, 2)), sems((SLOTS, 2)),
            sems((SLOTS, 4)), sems((SLOTS, 4)),
            sems((SLOTS,)), sems((SLOTS,)),
            sems((SLOTS, 2)), sems((SLOTS, 2)),
            sems((2, SLOTS)),
            sems((2,)),
        ],
        compiler_params=pltpu.CompilerParams(
            vmem_limit_bytes=61 * 2**20, collective_id=0, has_side_effects=True
        ),
    )(block_pairs.T, block_slot, emb, lab)
    out = ret.astype(F32) + (1.0 - ALPHA) * lab.astype(F32)
    return jnp.transpose(out.reshape(CLASSES, SLOTS, ROWS), (1, 0, 2))


def solution(mesh):
    return jax.shard_map(
        body,
        mesh=mesh,
        in_specs=(P("shard", None, None), P("shard", "rep", None), P(), P()),
        out_specs=P("shard", "rep", None),
        check_vma=False,
    )
```

```python
import functools
import math

import jax
import jax.numpy as jnp
from jax import lax
from jax.experimental import pallas as pl
from jax.experimental.pallas import tpu as pltpu
from jax.sharding import PartitionSpec as P

ITERS = 2
ALPHA = 0.9

SLOTS = 16
SIDE = 4
PAIRS = 40
ROWS = 512
DIM = 768
CLASSES = 125
PAD = 128
HALF = ROWS // 2
LANES = 128
UNROLL = 4
PAIR_UNROLL = 8
CHUNKS = ROWS // LANES
LEAD = 13

MESH = pl.DeviceIdType.MESH
NT = (((1,), (1,)), ((), ()))
NN = (((1,), (0,)), ((), ()))
BF = jnp.bfloat16
F32 = jnp.float32


def dot(a, b, dims):
    return lax.dot_general(a, b, dims, preferred_element_type=F32)


def main_kernel(
    pairs, slots, emb, lab, out,
    E, K, T, W, LT, SB, L, O, O2, R, SC, idx,
    se, re, sy, ry, sd, rd, sl, rl, sr, rr, so, loc,
):
    me = lax.axis_index("shard")
    rep = lax.axis_index("rep")
    y, core = rep // 2, rep % 2
    z, x = me // SIDE, me % SIDE
    up = ((y + 1) % SIDE) * 2 + core
    down = ((y + SIDE - 1) % SIDE) * 2 + core
    sibling = y * 2 + (1 - core)
    quarters = (y, (y + 2) % SIDE, (y + 3) % SIDE, (y + 1) % SIDE)

    def dest_of(u):
        return idx[u]

    def prev_of(u):
        return idx[2 * PAIRS + u]

    def last_of(s):
        return idx[4 * PAIRS + s]

    def offset(k):
        k = (k * 7) % SLOTS
        dz, dx = k // SIDE, k % SIDE
        return jnp.where(core == 0, dz, (SIDE - dx) % SIDE), jnp.where(core == 0, dx, (SIDE - dz) % SIDE)

    def to(k):
        dz, dx = offset(k)
        return ((z + dz) % SIDE) * SIDE + (x + dx) % SIDE

    def source(k):
        dz, dx = offset(k)
        return ((z + SIDE - dz) % SIDE) * SIDE + (x + SIDE - dx) % SIDE

    def remote(src, dst, send, recv, shard, r):
        return pltpu.make_async_remote_copy(
            src, dst, send, recv, device_id={"shard": shard, "rep": r}, device_id_type=MESH
        )

    def landing(g):
        return LT.at[pl.ds(g * PAD, PAD), :]

    def emb_copy(k, i):
        q = quarters[i]
        return remote(emb.at[to(k), q, core], E.at[me, q, core], se.at[k, i], re.at[k, i], to(k), rep)

    def y_copy(k, i):
        piece = E.at[source(k), quarters[0], core]
        return remote(piece, piece, sy.at[k, i], ry.at[k, i], me, (up, down)[i])

    def sib_copy(k, i):
        piece = E.at[source(k), quarters[i], core]
        return remote(piece, piece, sd.at[k, i], rd.at[k, i], me, sibling)

    def lab_copy(k):
        return remote(SB.at[to(k)], L.at[me], sl.at[k], rl.at[k], to(k), rep)

    def ret_copy(k, h):
        cols = pl.ds(h * LANES, LANES)
        return remote(
            SB.at[to(k), :, cols], landing(me).at[:, cols], sr.at[k, h], rr.at[k, h], to(k), rep
        )

    def ret_own(h):
        cols = pl.ds(h * LANES, LANES)
        return pltpu.make_async_copy(SB.at[me, :, cols], landing(me).at[:, cols], loc.at[h])

    def out_copies(h):
        cols = pl.ds(h * LANES, LANES)
        full = SLOTS * CLASSES // PAD
        rest = SLOTS * CLASSES - full * PAD
        yield from (
            pltpu.make_async_copy(O.at[i, :, cols], out.at[pl.ds(i * PAD, PAD), cols], so.at[h, i])
            for i in range(full)
        )
        yield pltpu.make_async_copy(
            O.at[full, pl.ds(0, rest), cols], out.at[pl.ds(full * PAD, rest), cols], so.at[h, full]
        )

    own_emb = pltpu.make_async_copy(emb.at[me], E.at[me], loc.at[0])
    own_lab = pltpu.make_async_copy(lab, LT.at[pl.ds(0, SLOTS * CLASSES), :], loc.at[1])
    own_emb.start()
    own_lab.start()

    barrier = pltpu.get_barrier_semaphore()

    @pl.loop(1, SLOTS)
    def _(k):
        pl.semaphore_signal(barrier, inc=1, device_id={"shard": to(k), "rep": rep}, device_id_type=MESH)

    for r in (up, down, sibling):
        pl.semaphore_signal(barrier, inc=1, device_id={"shard": me, "rep": r}, device_id_type=MESH)
    pl.semaphore_wait(barrier, SLOTS + 2)

    @pl.loop(1, SLOTS)
    def _(k):
        emb_copy(k, 0).start()

    @pl.loop(1, SLOTS)
    def _(k):
        emb_copy(k, 1).start()

    def walk(t, last):
        for end in range(2):
            u = 2 * t + end
            dest = slots[pairs[end, me * PAIRS + t]] // SLOTS
            idx[u] = dest
            prev = 2 * PAIRS
            for s in range(SLOTS):
                prev = jnp.where(dest == s, last[s], prev)
            idx[2 * PAIRS + u] = prev
            last = tuple(jnp.where(dest == s, u, last[s]) for s in range(SLOTS))
        return last

    last = lax.fori_loop(0, PAIRS, walk, (jnp.int32(2 * PAIRS),) * SLOTS)
    for s in range(SLOTS):
        idx[4 * PAIRS + s] = last[s]

    T[2 * PAIRS] = jnp.zeros((PAD, HALF), F32)
    R[2 * PAIRS] = jnp.zeros((1, ROWS), F32)

    own_lab.wait()
    for c in range(ROWS // LANES):
        cols = slice(c * LANES, (c + 1) * LANES)
        b = c % 2
        W[b, 0 : SLOTS * CLASSES, :] = LT[0 : SLOTS * CLASSES, cols].astype(F32)
        W[b, SLOTS * CLASSES : SLOTS * PAD, :] = jnp.zeros((SLOTS * (PAD - CLASSES), LANES), F32)
        for s in range(SLOTS):
            SB[s, :, cols] = W[b, pl.ds(s, PAD, stride=SLOTS), :].astype(BF)
    L[me] = SB[me]

    @pl.loop(1, SLOTS)
    def _(k):
        lab_copy(k).start()

    @pl.loop(1, SLOTS)
    def _(k):
        emb_copy(k, 0).wait_recv()
        y_copy(k, 0).start()
        y_copy(k, 1).start()
        sib_copy(k, 0).start()

    def second_half(k):
        y_copy(k, 0).wait_recv()
        y_copy(k, 1).wait_recv()
        sib_copy(k, 2).start()
        sib_copy(k, 3).start()
        emb_copy(k, 1).wait_recv()
        sib_copy(k, 1).start()

    pl.loop(1, LEAD)(second_half)

    pl.loop(LEAD, SLOTS)(second_half)

    @pl.loop(1, SLOTS)
    def _(k):
        for i in range(4):
            sib_copy(k, i).wait_recv()
    own_emb.wait()

    scale = math.log2(math.e) / math.sqrt(DIM)

    def tile(t):
        a = E[dest_of(2 * t)].reshape(ROWS, DIM)
        b = E[dest_of(2 * t + 1)].reshape(ROWS, DIM)
        kernel = jnp.exp2(dot(a, b, NT) * scale)
        K[t] = kernel.astype(BF)
        cols = jnp.sum(kernel, axis=0, keepdims=True)
        part = kernel[:, 0:128] + kernel[:, 128:256] + kernel[:, 256:384] + kernel[:, 384:512]
        rows = jnp.sum(part.T, axis=0, keepdims=True)
        for u, sums in ((2 * t, rows), (2 * t + 1, cols)):
            R[u] = sums + R[prev_of(u)]

    @pl.loop(0, PAIRS // UNROLL)
    def _(i):
        for j in range(UNROLL):
            tile(i * UNROLL + j)

    def scale_labels(s):
        scaling = 1.0 / jnp.sqrt(R[last_of(s)])
        SC[s] = scaling
        O[s] = (L[s].astype(F32) * scaling).astype(BF)

    scale_labels(me)

    @pl.loop(1, SLOTS)
    def _(k):
        lab_copy(k).wait()
        scale_labels(source(k))

    def products(src, start, width):
        cols = slice(start, start + width)

        def pair(t):
            first, second = dest_of(2 * t), dest_of(2 * t + 1)
            to_first = dot(src[second], K[t, cols, :], NT)
            to_second = dot(src[first], K[t, :, cols], NN)
            for u, product in ((2 * t, to_first), (2 * t + 1, to_second)):
                T[u, :, 0:width] = product + T[prev_of(u), :, 0:width]

        @pl.loop(0, PAIRS // PAIR_UNROLL)
        def _(i):
            for j in range(PAIR_UNROLL):
                pair(i * PAIR_UNROLL + j)

    for h in range(2):
        cols = slice(h * HALF, (h + 1) * HALF)
        products(O, h * HALF, HALF)

        @pl.loop(0, SLOTS)
        def _(s):
            scaling = SC[s, :, cols]
            field = (ALPHA * scaling) * T[last_of(s)] + (1.0 - ALPHA) * L[s, :, cols].astype(F32)
            O2[s, :, cols] = (field * scaling).astype(BF)

    for h in range(CHUNKS):
        cols = slice(h * LANES, (h + 1) * LANES)
        products(O2, h * LANES, LANES)

        def finish(s):
            SB[s, :, cols] = ((ALPHA * SC[s, :, cols]) * T[last_of(s), :, 0:LANES]).astype(BF)

        @pl.loop(1, SLOTS)
        def _(k):
            finish(to(k))
            ret_copy(k, h).start()

        finish(me)
        ret_own(h).start()

    @pl.loop(1, SLOTS)
    def _(k):
        for i in range(2):
            emb_copy(k, i).wait_send()
            y_copy(k, i).wait_send()
        for i in range(4):
            sib_copy(k, i).wait_send()

    for h in range(CHUNKS):
        @pl.loop(1, SLOTS)
        def _(k):
            ret_copy(k, h).wait()

        ret_own(h).wait()
        cols = slice(h * LANES, (h + 1) * LANES)
        b = h % 2
        for s in range(SLOTS):
            W[b, pl.ds(s, PAD, stride=SLOTS), :] = LT[s * PAD : (s + 1) * PAD, cols].astype(F32)
        for i in range(SLOTS):
            O[i, :, cols] = W[b, i * PAD : (i + 1) * PAD, :].astype(BF)
        for copy in out_copies(h):
            copy.start()

    for h in range(CHUNKS):
        for copy in out_copies(h):
            copy.wait()


def body(embeddings, labels, block_pairs, block_slot):
    emb = embeddings.reshape(SLOTS, SIDE, 2, ROWS // (2 * SIDE), DIM)
    lab = jnp.transpose(labels, (1, 0, 2)).reshape(CLASSES * SLOTS, ROWS)
    sems = pltpu.SemaphoreType.DMA
    ret = pl.pallas_call(
        main_kernel,
        out_shape=jax.ShapeDtypeStruct((CLASSES * SLOTS, ROWS), BF),
        in_specs=[
            pl.BlockSpec(memory_space=pltpu.SMEM),
            pl.BlockSpec(memory_space=pltpu.SMEM),
            pl.BlockSpec(memory_space=pl.ANY),
            pl.BlockSpec(memory_space=pl.ANY),
        ],
        out_specs=pl.BlockSpec(memory_space=pl.ANY),
        scratch_shapes=[
            pltpu.VMEM((SLOTS, SIDE, 2, ROWS // (2 * SIDE), DIM), BF),
            pltpu.VMEM((PAIRS, ROWS, ROWS), BF),
            pltpu.VMEM((2 * PAIRS + 1, PAD, HALF), F32),
            pltpu.VMEM((2, SLOTS * PAD, LANES), F32),
            pltpu.VMEM((SLOTS * PAD, ROWS), BF),
            pltpu.VMEM((SLOTS, PAD, ROWS), BF),
            pltpu.VMEM((SLOTS, PAD, ROWS), BF),
            pltpu.VMEM((SLOTS, PAD, ROWS), BF),
            pltpu.VMEM((SLOTS, PAD, ROWS), BF),
            pltpu.VMEM((2 * PAIRS + 1, 1, ROWS), F32),
            pltpu.VMEM((SLOTS, 1, ROWS), F32),
            pltpu.SMEM((4 * PAIRS + SLOTS,), jnp.int32),
            sems((SLOTS, 2)), sems((SLOTS, 2)),
            sems((SLOTS, 2)), sems((SLOTS, 2)),
            sems((SLOTS, 4)), sems((SLOTS, 4)),
            sems((SLOTS,)), sems((SLOTS,)),
            sems((SLOTS, CHUNKS)), sems((SLOTS, CHUNKS)),
            sems((CHUNKS, SLOTS)),
            sems((CHUNKS,)),
        ],
        compiler_params=pltpu.CompilerParams(
            vmem_limit_bytes=61 * 2**20, collective_id=0, has_side_effects=True
        ),
    )(block_pairs.T, block_slot, emb, lab)
    out = ret.astype(F32) + (1.0 - ALPHA) * lab.astype(F32)
    return jnp.transpose(out.reshape(CLASSES, SLOTS, ROWS), (1, 0, 2))


def solution(mesh):
    return jax.shard_map(
        body,
        mesh=mesh,
        in_specs=(P("shard", None, None), P("shard", "rep", None), P(), P()),
        out_specs=P("shard", "rep", None),
        check_vma=False,
    )
```

```python
import functools
import math

import jax
import jax.numpy as jnp
from jax import lax
from jax.experimental import pallas as pl
from jax.experimental.pallas import tpu as pltpu
from jax.sharding import PartitionSpec as P

ITERS = 2
ALPHA = 0.9

SLOTS = 16
SIDE = 4
PAIRS = 40
ROWS = 512
DIM = 768
CLASSES = 125
PAD = 128
HALF = ROWS // 2
LANES = 128
UNROLL = 8
PAIR_UNROLL = 8
CHUNKS = ROWS // LANES

MESH = pl.DeviceIdType.MESH
NT = (((1,), (1,)), ((), ()))
NN = (((1,), (0,)), ((), ()))
BF = jnp.bfloat16
F32 = jnp.float32


def dot(a, b, dims):
    return lax.dot_general(a, b, dims, preferred_element_type=F32)


def main_kernel(
    pairs, slots, emb, lab, out,
    E, K, T, W, LT, SB, L, O, O2, R, SC, idx,
    se, re, sy, ry, sd, rd, sl, rl, sr, rr, so, loc,
):
    me = lax.axis_index("shard")
    rep = lax.axis_index("rep")
    y, core = rep // 2, rep % 2
    z, x = me // SIDE, me % SIDE
    up = ((y + 1) % SIDE) * 2 + core
    down = ((y + SIDE - 1) % SIDE) * 2 + core
    sibling = y * 2 + (1 - core)
    quarters = (y, (y + 2) % SIDE)

    def dest_of(u):
        return idx[u]

    def prev_of(u):
        return idx[2 * PAIRS + u]

    def last_of(s):
        return idx[4 * PAIRS + s]

    def offset(k):
        k = (k * 7) % SLOTS
        dz, dx = k // SIDE, k % SIDE
        return jnp.where(core == 0, dz, (SIDE - dx) % SIDE), jnp.where(core == 0, dx, (SIDE - dz) % SIDE)

    def to(k):
        dz, dx = offset(k)
        return ((z + dz) % SIDE) * SIDE + (x + dx) % SIDE

    def source(k):
        dz, dx = offset(k)
        return ((z + SIDE - dz) % SIDE) * SIDE + (x + SIDE - dx) % SIDE

    def remote(src, dst, send, recv, shard, r):
        return pltpu.make_async_remote_copy(
            src, dst, send, recv, device_id={"shard": shard, "rep": r}, device_id_type=MESH
        )

    def landing(g):
        return LT.at[pl.ds(g * PAD, PAD), :]

    def emb_copy(k, i):
        q = quarters[i]
        return remote(emb.at[to(k), q, core], E.at[me, q, core], se.at[k, i], re.at[k, i], to(k), rep)

    def y_copy(k, i):
        piece = E.at[source(k), quarters[0], core]
        return remote(piece, piece, sy.at[k, i], ry.at[k, i], me, (up, down)[i])

    def sib_copy(k):
        piece = E.at[source(k), :, core]
        return remote(piece, piece, sd.at[k], rd.at[k], me, sibling)

    def lab_copy(k):
        return remote(SB.at[to(k)], L.at[me], sl.at[k], rl.at[k], to(k), rep)

    def ret_copy(k, h):
        cols = pl.ds(h * LANES, LANES)
        return remote(
            SB.at[to(k), :, cols], landing(me).at[:, cols], sr.at[k, h], rr.at[k, h], to(k), rep
        )

    def ret_own(h):
        cols = pl.ds(h * LANES, LANES)
        return pltpu.make_async_copy(SB.at[me, :, cols], landing(me).at[:, cols], loc.at[h])

    def out_copies(h):
        cols = pl.ds(h * LANES, LANES)
        full = SLOTS * CLASSES // PAD
        rest = SLOTS * CLASSES - full * PAD
        yield from (
            pltpu.make_async_copy(O.at[i, :, cols], out.at[pl.ds(i * PAD, PAD), cols], so.at[h, i])
            for i in range(full)
        )
        yield pltpu.make_async_copy(
            O.at[full, pl.ds(0, rest), cols], out.at[pl.ds(full * PAD, rest), cols], so.at[h, full]
        )

    own_emb = pltpu.make_async_copy(emb.at[me], E.at[me], loc.at[0])
    own_lab = pltpu.make_async_copy(lab, LT.at[pl.ds(0, SLOTS * CLASSES), :], loc.at[1])
    own_emb.start()
    own_lab.start()

    barrier = pltpu.get_barrier_semaphore()

    @pl.loop(1, SLOTS)
    def _(k):
        pl.semaphore_signal(barrier, inc=1, device_id={"shard": to(k), "rep": rep}, device_id_type=MESH)

    for r in (up, down, sibling):
        pl.semaphore_signal(barrier, inc=1, device_id={"shard": me, "rep": r}, device_id_type=MESH)
    pl.semaphore_wait(barrier, SLOTS + 2)

    @pl.loop(1, SLOTS)
    def _(k):
        emb_copy(k, 0).start()

    @pl.loop(1, SLOTS)
    def _(k):
        emb_copy(k, 1).start()

    T[2 * PAIRS] = jnp.zeros((PAD, HALF), F32)
    R[2 * PAIRS] = jnp.zeros((1, ROWS), F32)

    @pl.loop(1, SLOTS)
    def _(k):
        emb_copy(k, 0).wait_recv()
        y_copy(k, 0).start()
        y_copy(k, 1).start()

    own_lab.wait()
    for c in range(ROWS // LANES):
        cols = slice(c * LANES, (c + 1) * LANES)
        b = c % 2
        W[b, 0 : SLOTS * CLASSES, :] = LT[0 : SLOTS * CLASSES, cols].astype(F32)
        W[b, SLOTS * CLASSES : SLOTS * PAD, :] = jnp.zeros((SLOTS * (PAD - CLASSES), LANES), F32)
        for s in range(SLOTS):
            SB[s, :, cols] = W[b, pl.ds(s, PAD, stride=SLOTS), :].astype(BF)
    L[me] = SB[me]

    @pl.loop(1, SLOTS)
    def _(k):
        lab_copy(k).start()

    def walk(t, last):
        for end in range(2):
            u = 2 * t + end
            dest = slots[pairs[end, me * PAIRS + t]] // SLOTS
            idx[u] = dest
            prev = 2 * PAIRS
            for s in range(SLOTS):
                prev = jnp.where(dest == s, last[s], prev)
            idx[2 * PAIRS + u] = prev
            last = tuple(jnp.where(dest == s, u, last[s]) for s in range(SLOTS))
        return last

    last = lax.fori_loop(0, PAIRS, walk, (jnp.int32(2 * PAIRS),) * SLOTS)
    for s in range(SLOTS):
        idx[4 * PAIRS + s] = last[s]

    def second_half(k):
        y_copy(k, 0).wait_recv()
        y_copy(k, 1).wait_recv()
        emb_copy(k, 1).wait_recv()
        sib_copy(k).start()

    pl.loop(1, SLOTS)(second_half)

    @pl.loop(1, SLOTS)
    def _(k):
        sib_copy(k).wait_recv()
    own_emb.wait()

    scale = math.log2(math.e) / math.sqrt(DIM)

    def tile(t):
        a = E[dest_of(2 * t)].reshape(ROWS, DIM)
        b = E[dest_of(2 * t + 1)].reshape(ROWS, DIM)
        kernel = jnp.exp2(dot(a, b, NT) * scale)
        K[t] = kernel.astype(BF)
        cols = jnp.sum(kernel, axis=0, keepdims=True)
        part = kernel[:, 0:128] + kernel[:, 128:256] + kernel[:, 256:384] + kernel[:, 384:512]
        rows = jnp.sum(part.T, axis=0, keepdims=True)
        for u, sums in ((2 * t, rows), (2 * t + 1, cols)):
            R[u] = sums + R[prev_of(u)]

    @pl.loop(0, PAIRS // UNROLL)
    def _(i):
        for j in range(UNROLL):
            tile(i * UNROLL + j)

    def scale_labels(s):
        scaling = 1.0 / jnp.sqrt(R[last_of(s)])
        SC[s] = scaling
        O[s] = (L[s].astype(F32) * scaling).astype(BF)

    scale_labels(me)

    @pl.loop(1, SLOTS)
    def _(k):
        lab_copy(k).wait()
        scale_labels(source(k))

    def products(src, start, width):
        cols = slice(start, start + width)

        def pair(t):
            first, second = dest_of(2 * t), dest_of(2 * t + 1)
            to_first = dot(src[second], K[t, cols, :], NT)
            to_second = dot(src[first], K[t, :, cols], NN)
            for u, product in ((2 * t, to_first), (2 * t + 1, to_second)):
                T[u, :, 0:width] = product + T[prev_of(u), :, 0:width]

        @pl.loop(0, PAIRS // PAIR_UNROLL)
        def _(i):
            for j in range(PAIR_UNROLL):
                pair(i * PAIR_UNROLL + j)

    for h in range(2):
        cols = slice(h * HALF, (h + 1) * HALF)
        products(O, h * HALF, HALF)

        @pl.loop(0, SLOTS)
        def _(s):
            scaling = SC[s, :, cols]
            field = (ALPHA * scaling) * T[last_of(s)] + (1.0 - ALPHA) * L[s, :, cols].astype(F32)
            O2[s, :, cols] = (field * scaling).astype(BF)

    for h in range(CHUNKS):
        cols = slice(h * LANES, (h + 1) * LANES)
        products(O2, h * LANES, LANES)

        def finish(s):
            SB[s, :, cols] = ((ALPHA * SC[s, :, cols]) * T[last_of(s), :, 0:LANES]).astype(BF)

        @pl.loop(1, SLOTS)
        def _(k):
            finish(to(k))
            ret_copy(k, h).start()

        finish(me)
        ret_own(h).start()

    @pl.loop(1, SLOTS)
    def _(k):
        for i in range(2):
            emb_copy(k, i).wait_send()
            y_copy(k, i).wait_send()
        sib_copy(k).wait_send()

    for h in range(CHUNKS):
        @pl.loop(1, SLOTS)
        def _(k):
            ret_copy(k, h).wait()

        ret_own(h).wait()
        cols = slice(h * LANES, (h + 1) * LANES)
        b = h % 2
        for s in range(SLOTS):
            W[b, pl.ds(s, PAD, stride=SLOTS), :] = LT[s * PAD : (s + 1) * PAD, cols].astype(F32)
        for i in range(SLOTS):
            O[i, :, cols] = W[b, i * PAD : (i + 1) * PAD, :].astype(BF)
        for copy in out_copies(h):
            copy.start()

    for h in range(CHUNKS):
        for copy in out_copies(h):
            copy.wait()


def body(embeddings, labels, block_pairs, block_slot):
    emb = embeddings.reshape(SLOTS, SIDE, 2, ROWS // (2 * SIDE), DIM)
    lab = jnp.transpose(labels, (1, 0, 2)).reshape(CLASSES * SLOTS, ROWS)
    sems = pltpu.SemaphoreType.DMA
    ret = pl.pallas_call(
        main_kernel,
        out_shape=jax.ShapeDtypeStruct((CLASSES * SLOTS, ROWS), BF),
        in_specs=[
            pl.BlockSpec(memory_space=pltpu.SMEM),
            pl.BlockSpec(memory_space=pltpu.SMEM),
            pl.BlockSpec(memory_space=pltpu.HBM),
            pl.BlockSpec(memory_space=pltpu.HBM),
        ],
        out_specs=pl.BlockSpec(memory_space=pl.ANY),
        scratch_shapes=[
            pltpu.VMEM((SLOTS, SIDE, 2, ROWS // (2 * SIDE), DIM), BF),
            pltpu.VMEM((PAIRS, ROWS, ROWS), BF),
            pltpu.VMEM((2 * PAIRS + 1, PAD, HALF), F32),
            pltpu.VMEM((2, SLOTS * PAD, LANES), F32),
            pltpu.VMEM((SLOTS * PAD, ROWS), BF),
            pltpu.VMEM((SLOTS, PAD, ROWS), BF),
            pltpu.VMEM((SLOTS, PAD, ROWS), BF),
            pltpu.VMEM((SLOTS, PAD, ROWS), BF),
            pltpu.VMEM((SLOTS, PAD, ROWS), BF),
            pltpu.VMEM((2 * PAIRS + 1, 1, ROWS), F32),
            pltpu.VMEM((SLOTS, 1, ROWS), F32),
            pltpu.SMEM((4 * PAIRS + SLOTS,), jnp.int32),
            sems((SLOTS, 2)), sems((SLOTS, 2)),
            sems((SLOTS, 2)), sems((SLOTS, 2)),
            sems((SLOTS,)), sems((SLOTS,)),
            sems((SLOTS,)), sems((SLOTS,)),
            sems((SLOTS, CHUNKS)), sems((SLOTS, CHUNKS)),
            sems((CHUNKS, SLOTS)),
            sems((CHUNKS,)),
        ],
        compiler_params=pltpu.CompilerParams(
            vmem_limit_bytes=58 * 2**20, collective_id=0, has_side_effects=True
        ),
    )(block_pairs.T, block_slot, emb, lab)
    out = ret.astype(F32) + (1.0 - ALPHA) * lab.astype(F32)
    return jnp.transpose(out.reshape(CLASSES, SLOTS, ROWS), (1, 0, 2))


def solution(mesh):
    return jax.shard_map(
        body,
        mesh=mesh,
        in_specs=(P("shard", None, None), P("shard", "rep", None), P(), P()),
        out_specs=P("shard", "rep", None),
        check_vma=False,
    )
```

```python
import functools
import math

import jax
import jax.numpy as jnp
from jax import lax
from jax.experimental import pallas as pl
from jax.experimental.pallas import tpu as pltpu
from jax.sharding import PartitionSpec as P

ITERS = 2
ALPHA = 0.9

SLOTS = 16
SIDE = 4
PAIRS = 40
ROWS = 512
DIM = 768
CLASSES = 125
PAD = 128
HALF = ROWS // 2
LANES = 128
UNROLL = 8
PAIR_UNROLL = 8
CHUNKS = ROWS // LANES

MESH = pl.DeviceIdType.MESH
NT = (((1,), (1,)), ((), ()))
NN = (((1,), (0,)), ((), ()))
BF = jnp.bfloat16
F32 = jnp.float32


def dot(a, b, dims):
    return lax.dot_general(a, b, dims, preferred_element_type=F32)


def main_kernel(
    pairs, slots, emb, lab, out,
    EA, EB, S, K, T, W, LT, SB, L, O, O2, R, SC, idx,
    se, re, sy, ry, sd, rd, sl, rl, sr, rr, so, loc,
):
    me = lax.axis_index("shard")
    rep = lax.axis_index("rep")
    y, core = rep // 2, rep % 2
    z, x = me // SIDE, me % SIDE
    up = ((y + 1) % SIDE) * 2 + core
    down = ((y + SIDE - 1) % SIDE) * 2 + core
    sibling = y * 2 + (1 - core)
    quarters = (y, (y + 2) % SIDE)

    def dest_of(u):
        return idx[u]

    def prev_of(u):
        return idx[2 * PAIRS + u]

    def last_of(s):
        return idx[4 * PAIRS + s]

    def offset(k):
        k = (k * 7) % SLOTS
        dz, dx = k // SIDE, k % SIDE
        return jnp.where(core == 0, dz, (SIDE - dx) % SIDE), jnp.where(core == 0, dx, (SIDE - dz) % SIDE)

    def to(k):
        dz, dx = offset(k)
        return ((z + dz) % SIDE) * SIDE + (x + dx) % SIDE

    def source(k):
        dz, dx = offset(k)
        return ((z + SIDE - dz) % SIDE) * SIDE + (x + SIDE - dx) % SIDE

    def remote(src, dst, send, recv, shard, r):
        return pltpu.make_async_remote_copy(
            src, dst, send, recv, device_id={"shard": shard, "rep": r}, device_id_type=MESH
        )

    def landing(g):
        return LT.at[pl.ds(g * PAD, PAD), :]

    halves = (EA, EB)

    def emb_copy(p, k, i):
        q = quarters[i]
        return remote(
            emb.at[to(k), p, q, core], halves[p].at[me, q, core], se.at[p, k, i], re.at[p, k, i], to(k), rep
        )

    def y_copy(p, k, i):
        piece = halves[p].at[source(k), y, core]
        return remote(piece, piece, sy.at[p, k, i], ry.at[p, k, i], me, (up, down)[i])

    def sib_copy(p, k):
        piece = halves[p].at[source(k), :, core]
        return remote(piece, piece, sd.at[p, k], rd.at[p, k], me, sibling)

    def own_emb(p):
        return pltpu.make_async_copy(emb.at[me, p], halves[p].at[me], loc.at[2 * p])

    def lab_copy(k):
        return remote(SB.at[to(k)], L.at[me], sl.at[k], rl.at[k], to(k), rep)

    def ret_copy(k, h):
        cols = pl.ds(h * LANES, LANES)
        return remote(
            SB.at[to(k), :, cols], landing(me).at[:, cols], sr.at[k, h], rr.at[k, h], to(k), rep
        )

    def ret_own(h):
        cols = pl.ds(h * LANES, LANES)
        return pltpu.make_async_copy(SB.at[me, :, cols], landing(me).at[:, cols], loc.at[h])

    def out_copies(h):
        cols = pl.ds(h * LANES, LANES)
        full = SLOTS * CLASSES // PAD
        rest = SLOTS * CLASSES - full * PAD
        yield from (
            pltpu.make_async_copy(O.at[i, :, cols], out.at[pl.ds(i * PAD, PAD), cols], so.at[h, i])
            for i in range(full)
        )
        yield pltpu.make_async_copy(
            O.at[full, pl.ds(0, rest), cols], out.at[pl.ds(full * PAD, rest), cols], so.at[h, full]
        )

    own_lab = pltpu.make_async_copy(lab, LT.at[pl.ds(0, SLOTS * CLASSES), :], loc.at[1])
    own_emb(0).start()
    own_emb(1).start()
    own_lab.start()

    barrier = pltpu.get_barrier_semaphore()

    @pl.loop(1, SLOTS)
    def _(k):
        pl.semaphore_signal(barrier, inc=1, device_id={"shard": to(k), "rep": rep}, device_id_type=MESH)

    for r in (up, down, sibling):
        pl.semaphore_signal(barrier, inc=1, device_id={"shard": me, "rep": r}, device_id_type=MESH)
    pl.semaphore_wait(barrier, SLOTS + 2)

    for p in range(2):
        for i in range(2):
            @pl.loop(1, SLOTS)
            def _(k):
                emb_copy(p, k, i).start()

    def forward(p, k):
        emb_copy(p, k, 0).wait_recv()
        y_copy(p, k, 0).start()
        y_copy(p, k, 1).start()

    def share(p):
        @pl.loop(1, SLOTS)
        def _(k):
            y_copy(p, k, 0).wait_recv()
            y_copy(p, k, 1).wait_recv()
            emb_copy(p, k, 1).wait_recv()
            sib_copy(p, k).start()

        @pl.loop(1, SLOTS)
        def _(k):
            sib_copy(p, k).wait_recv()

        own_emb(p).wait()

    T[2 * PAIRS] = jnp.zeros((PAD, HALF), F32)
    R[2 * PAIRS] = jnp.zeros((1, ROWS), F32)

    @pl.loop(1, SLOTS)
    def _(k):
        forward(0, k)

    own_lab.wait()
    for c in range(ROWS // LANES):
        cols = slice(c * LANES, (c + 1) * LANES)
        b = c % 2
        W[b, 0 : SLOTS * CLASSES, :] = LT[0 : SLOTS * CLASSES, cols].astype(F32)
        W[b, SLOTS * CLASSES : SLOTS * PAD, :] = jnp.zeros((SLOTS * (PAD - CLASSES), LANES), F32)
        for s in range(SLOTS):
            SB[s, :, cols] = W[b, pl.ds(s, PAD, stride=SLOTS), :].astype(BF)
    L[me] = SB[me]

    @pl.loop(1, SLOTS)
    def _(k):
        lab_copy(k).start()

    def walk(t, last):
        for end in range(2):
            u = 2 * t + end
            dest = slots[pairs[end, me * PAIRS + t]] // SLOTS
            idx[u] = dest
            prev = 2 * PAIRS
            for s in range(SLOTS):
                prev = jnp.where(dest == s, last[s], prev)
            idx[2 * PAIRS + u] = prev
            last = tuple(jnp.where(dest == s, u, last[s]) for s in range(SLOTS))
        return last

    last = lax.fori_loop(0, PAIRS, walk, (jnp.int32(2 * PAIRS),) * SLOTS)
    for s in range(SLOTS):
        idx[4 * PAIRS + s] = last[s]

    share(0)

    scale = math.log2(math.e) / math.sqrt(DIM)

    def load(ref, u):
        return ref[dest_of(u)].reshape(HALF, DIM)

    def corner(t):
        kernel = jnp.exp2(dot(load(EA, 2 * t), load(EA, 2 * t + 1), NT) * scale)
        K[t, 0:HALF, 0:HALF] = kernel.astype(BF)
        S[2 * t + 1] = jnp.sum(kernel, axis=0, keepdims=True)
        S[2 * t] = jnp.sum((kernel[:, 0:128] + kernel[:, 128:256]).T, axis=0, keepdims=True)

    def rest(t):
        low_a, high_a = load(EA, 2 * t), load(EB, 2 * t)
        low_b, high_b = load(EA, 2 * t + 1), load(EB, 2 * t + 1)
        right = jnp.exp2(dot(jnp.concatenate([low_a, high_a], axis=0), high_b, NT) * scale)
        K[t, :, HALF:ROWS] = right.astype(BF)
        left = jnp.exp2(dot(high_a, low_b, NT) * scale)
        K[t, HALF:ROWS, 0:HALF] = left.astype(BF)
        part = right[:, 0:128] + right[:, 128:256]
        high_part = part[HALF:ROWS] + left[:, 0:128] + left[:, 128:256]
        low_rows = jnp.sum(part[0:HALF].T, axis=0, keepdims=True) + S[2 * t]
        high_rows = jnp.sum(high_part.T, axis=0, keepdims=True)
        low_cols = jnp.sum(left, axis=0, keepdims=True) + S[2 * t + 1]
        high_cols = jnp.sum(right, axis=0, keepdims=True)
        for u, low, high in ((2 * t, low_rows, high_rows), (2 * t + 1, low_cols, high_cols)):
            prev = prev_of(u)
            R[u, :, 0:HALF] = low + R[prev, :, 0:HALF]
            R[u, :, HALF:ROWS] = high + R[prev, :, HALF:ROWS]

    steps = PAIRS // UNROLL
    share_of_step = (SLOTS - 1) // steps

    @pl.loop(0, steps)
    def _(i):
        for j in range(share_of_step):
            forward(1, 1 + i * share_of_step + j)
        for j in range(UNROLL):
            corner(i * UNROLL + j)

    share(1)

    @pl.loop(0, steps)
    def _(i):
        for j in range(UNROLL):
            rest(i * UNROLL + j)

    def scale_labels(s):
        scaling = 1.0 / jnp.sqrt(R[last_of(s)])
        SC[s] = scaling
        O[s] = (L[s].astype(F32) * scaling).astype(BF)

    scale_labels(me)

    @pl.loop(1, SLOTS)
    def _(k):
        lab_copy(k).wait()
        scale_labels(source(k))

    def products(src, start, width):
        cols = slice(start, start + width)

        def pair(t):
            first, second = dest_of(2 * t), dest_of(2 * t + 1)
            to_first = dot(src[second], K[t, cols, :], NT)
            to_second = dot(src[first], K[t, :, cols], NN)
            for u, product in ((2 * t, to_first), (2 * t + 1, to_second)):
                T[u, :, 0:width] = product + T[prev_of(u), :, 0:width]

        @pl.loop(0, PAIRS // PAIR_UNROLL)
        def _(i):
            for j in range(PAIR_UNROLL):
                pair(i * PAIR_UNROLL + j)

    for h in range(2):
        cols = slice(h * HALF, (h + 1) * HALF)
        products(O, h * HALF, HALF)

        @pl.loop(0, SLOTS)
        def _(s):
            scaling = SC[s, :, cols]
            field = (ALPHA * scaling) * T[last_of(s)] + (1.0 - ALPHA) * L[s, :, cols].astype(F32)
            O2[s, :, cols] = (field * scaling).astype(BF)

    for h in range(CHUNKS):
        cols = slice(h * LANES, (h + 1) * LANES)
        products(O2, h * LANES, LANES)

        def finish(s):
            SB[s, :, cols] = ((ALPHA * SC[s, :, cols]) * T[last_of(s), :, 0:LANES]).astype(BF)

        @pl.loop(1, SLOTS)
        def _(k):
            finish(to(k))
            ret_copy(k, h).start()

        finish(me)
        ret_own(h).start()

    @pl.loop(1, SLOTS)
    def _(k):
        for p in range(2):
            for i in range(2):
                emb_copy(p, k, i).wait_send()
                y_copy(p, k, i).wait_send()
            sib_copy(p, k).wait_send()

    for h in range(CHUNKS):
        @pl.loop(1, SLOTS)
        def _(k):
            ret_copy(k, h).wait()

        ret_own(h).wait()
        cols = slice(h * LANES, (h + 1) * LANES)
        b = h % 2
        for s in range(SLOTS):
            W[b, pl.ds(s, PAD, stride=SLOTS), :] = LT[s * PAD : (s + 1) * PAD, cols].astype(F32)
        for i in range(SLOTS):
            O[i, :, cols] = W[b, i * PAD : (i + 1) * PAD, :].astype(BF)
        for copy in out_copies(h):
            copy.start()

    for h in range(CHUNKS):
        for copy in out_copies(h):
            copy.wait()


def body(embeddings, labels, block_pairs, block_slot):
    emb = embeddings.reshape(SLOTS, 2, SIDE, 2, HALF // (2 * SIDE), DIM)
    lab = jnp.transpose(labels, (1, 0, 2)).reshape(CLASSES * SLOTS, ROWS)
    sems = pltpu.SemaphoreType.DMA
    ret = pl.pallas_call(
        main_kernel,
        out_shape=jax.ShapeDtypeStruct((CLASSES * SLOTS, ROWS), BF),
        in_specs=[
            pl.BlockSpec(memory_space=pltpu.SMEM),
            pl.BlockSpec(memory_space=pltpu.SMEM),
            pl.BlockSpec(memory_space=pltpu.HBM),
            pl.BlockSpec(memory_space=pltpu.HBM),
        ],
        out_specs=pl.BlockSpec(memory_space=pl.ANY),
        scratch_shapes=[
            pltpu.VMEM((SLOTS, SIDE, 2, HALF // (2 * SIDE), DIM), BF),
            pltpu.VMEM((SLOTS, SIDE, 2, HALF // (2 * SIDE), DIM), BF),
            pltpu.VMEM((2 * PAIRS, 1, HALF), F32),
            pltpu.VMEM((PAIRS, ROWS, ROWS), BF),
            pltpu.VMEM((2 * PAIRS + 1, PAD, HALF), F32),
            pltpu.VMEM((2, SLOTS * PAD, LANES), F32),
            pltpu.VMEM((SLOTS * PAD, ROWS), BF),
            pltpu.VMEM((SLOTS, PAD, ROWS), BF),
            pltpu.VMEM((SLOTS, PAD, ROWS), BF),
            pltpu.VMEM((SLOTS, PAD, ROWS), BF),
            pltpu.VMEM((SLOTS, PAD, ROWS), BF),
            pltpu.VMEM((2 * PAIRS + 1, 1, ROWS), F32),
            pltpu.VMEM((SLOTS, 1, ROWS), F32),
            pltpu.SMEM((4 * PAIRS + SLOTS,), jnp.int32),
            sems((2, SLOTS, 2)), sems((2, SLOTS, 2)),
            sems((2, SLOTS, 2)), sems((2, SLOTS, 2)),
            sems((2, SLOTS)), sems((2, SLOTS)),
            sems((SLOTS,)), sems((SLOTS,)),
            sems((SLOTS, CHUNKS)), sems((SLOTS, CHUNKS)),
            sems((CHUNKS, SLOTS)),
            sems((CHUNKS,)),
        ],
        compiler_params=pltpu.CompilerParams(
            vmem_limit_bytes=58 * 2**20, collective_id=0, has_side_effects=True
        ),
    )(block_pairs.T, block_slot, emb, lab)
    out = ret.astype(F32) + (1.0 - ALPHA) * lab.astype(F32)
    return jnp.transpose(out.reshape(CLASSES, SLOTS, ROWS), (1, 0, 2))


def solution(mesh):
    return jax.shard_map(
        body,
        mesh=mesh,
        in_specs=(P("shard", None, None), P("shard", "rep", None), P(), P()),
        out_specs=P("shard", "rep", None),
        check_vma=False,
    )
```

```python
import functools
import math

import jax
import jax.numpy as jnp
from jax import lax
from jax.experimental import pallas as pl
from jax.experimental.pallas import tpu as pltpu
from jax.sharding import PartitionSpec as P

ITERS = 2
ALPHA = 0.9

SLOTS = 16
SIDE = 4
PAIRS = 40
ROWS = 512
DIM = 768
CLASSES = 125
PAD = 128
HALF = ROWS // 2
LANES = 128
UNROLL = 8
PAIR_UNROLL = 8
CHUNKS = ROWS // LANES

MESH = pl.DeviceIdType.MESH
NT = (((1,), (1,)), ((), ()))
NN = (((1,), (0,)), ((), ()))
BF = jnp.bfloat16
F32 = jnp.float32


def dot(a, b, dims):
    return lax.dot_general(a, b, dims, preferred_element_type=F32)


def main_kernel(
    pairs, slots, emb, lab, out,
    EA, EB, S, K, T, W, LT, SB, L, O, O2, R, SC, idx,
    se, re, sy, ry, sd, rd, sp, rp, sl, rl, sr, rr, so, loc,
):
    me = lax.axis_index("shard")
    rep = lax.axis_index("rep")
    y, core = rep // 2, rep % 2
    z, x = me // SIDE, me % SIDE
    up = ((y + 1) % SIDE) * 2 + core
    down = ((y + SIDE - 1) % SIDE) * 2 + core
    sibling = y * 2 + (1 - core)
    quarters = (y, (y + 2) % SIDE)

    def dest_of(u):
        return idx[u]

    def prev_of(u):
        return idx[2 * PAIRS + u]

    def last_of(s):
        return idx[4 * PAIRS + s]

    def offset(k):
        k = (k * 7) % SLOTS
        dz, dx = k // SIDE, k % SIDE
        return jnp.where(core == 0, dz, (SIDE - dx) % SIDE), jnp.where(core == 0, dx, (SIDE - dz) % SIDE)

    def to(k):
        dz, dx = offset(k)
        return ((z + dz) % SIDE) * SIDE + (x + dx) % SIDE

    def source(k):
        dz, dx = offset(k)
        return ((z + SIDE - dz) % SIDE) * SIDE + (x + SIDE - dx) % SIDE

    def remote(src, dst, send, recv, shard, r):
        return pltpu.make_async_remote_copy(
            src, dst, send, recv, device_id={"shard": shard, "rep": r}, device_id_type=MESH
        )

    def landing(g):
        return LT.at[pl.ds(g * PAD, PAD), :]

    halves = (EA, EB)

    def emb_copy(p, k, i):
        q = quarters[i]
        return remote(
            emb.at[to(k), p, q, core], halves[p].at[me, q, core], se.at[p, k, i], re.at[p, k, i], to(k), rep
        )

    def y_copy(p, k, i):
        piece = halves[p].at[source(k), y, core]
        return remote(piece, piece, sy.at[p, k, i], ry.at[p, k, i], me, (up, down)[i])

    def pass_copy(k):
        q = jnp.where(core == 0, (y + 1) % SIDE, (y + SIDE - 1) % SIDE)
        piece = EB.at[source(k), q, core]
        return remote(piece, piece, sp.at[k], rp.at[k], me, jnp.where(core == 0, down, up))

    def sib_copy(p, k):
        piece = halves[p].at[source(k), :, core]
        return remote(piece, piece, sd.at[p, k], rd.at[p, k], me, sibling)

    def own_emb(p):
        return pltpu.make_async_copy(emb.at[me, p], halves[p].at[me], loc.at[2 * p])

    def lab_copy(k):
        return remote(SB.at[to(k)], L.at[me], sl.at[k], rl.at[k], to(k), rep)

    def ret_copy(k, h):
        cols = pl.ds(h * LANES, LANES)
        return remote(
            SB.at[to(k), :, cols], landing(me).at[:, cols], sr.at[k, h], rr.at[k, h], to(k), rep
        )

    def ret_own(h):
        cols = pl.ds(h * LANES, LANES)
        return pltpu.make_async_copy(SB.at[me, :, cols], landing(me).at[:, cols], loc.at[h])

    def out_copies(h):
        cols = pl.ds(h * LANES, LANES)
        full = SLOTS * CLASSES // PAD
        rest = SLOTS * CLASSES - full * PAD
        yield from (
            pltpu.make_async_copy(O.at[i, :, cols], out.at[pl.ds(i * PAD, PAD), cols], so.at[h, i])
            for i in range(full)
        )
        yield pltpu.make_async_copy(
            O.at[full, pl.ds(0, rest), cols], out.at[pl.ds(full * PAD, rest), cols], so.at[h, full]
        )

    own_lab = pltpu.make_async_copy(lab, LT.at[pl.ds(0, SLOTS * CLASSES), :], loc.at[1])
    own_emb(0).start()
    own_emb(1).start()
    own_lab.start()

    barrier = pltpu.get_barrier_semaphore()

    @pl.loop(1, SLOTS)
    def _(k):
        pl.semaphore_signal(barrier, inc=1, device_id={"shard": to(k), "rep": rep}, device_id_type=MESH)

    for r in (up, down, sibling):
        pl.semaphore_signal(barrier, inc=1, device_id={"shard": me, "rep": r}, device_id_type=MESH)
    pl.semaphore_wait(barrier, SLOTS + 2)

    for p, i in ((0, 0), (0, 1), (1, 0)):
        @pl.loop(1, SLOTS)
        def _(k):
            emb_copy(p, k, i).start()

    def forward(p, k):
        emb_copy(p, k, 0).wait_recv()
        y_copy(p, k, 0).start()
        y_copy(p, k, 1).start()

    def share(p):
        @pl.loop(1, SLOTS)
        def _(k):
            y_copy(p, k, 0).wait_recv()
            y_copy(p, k, 1).wait_recv()
            if p == 0:
                emb_copy(p, k, 1).wait_recv()
                sib_copy(p, k).start()
            else:
                pass_copy(k).start()

        if p == 1:
            @pl.loop(1, SLOTS)
            def _(k):
                pass_copy(k).wait_recv()
                sib_copy(p, k).start()

        @pl.loop(1, SLOTS)
        def _(k):
            sib_copy(p, k).wait_recv()

        own_emb(p).wait()

    T[2 * PAIRS] = jnp.zeros((PAD, HALF), F32)
    R[2 * PAIRS] = jnp.zeros((1, ROWS), F32)

    @pl.loop(1, SLOTS)
    def _(k):
        forward(0, k)

    own_lab.wait()
    for c in range(ROWS // LANES):
        cols = slice(c * LANES, (c + 1) * LANES)
        b = c % 2
        W[b, 0 : SLOTS * CLASSES, :] = LT[0 : SLOTS * CLASSES, cols].astype(F32)
        W[b, SLOTS * CLASSES : SLOTS * PAD, :] = jnp.zeros((SLOTS * (PAD - CLASSES), LANES), F32)
        for s in range(SLOTS):
            SB[s, :, cols] = W[b, pl.ds(s, PAD, stride=SLOTS), :].astype(BF)
    L[me] = SB[me]

    @pl.loop(1, SLOTS)
    def _(k):
        lab_copy(k).start()

    def walk(t, last):
        for end in range(2):
            u = 2 * t + end
            dest = slots[pairs[end, me * PAIRS + t]] // SLOTS
            idx[u] = dest
            prev = 2 * PAIRS
            for s in range(SLOTS):
                prev = jnp.where(dest == s, last[s], prev)
            idx[2 * PAIRS + u] = prev
            last = tuple(jnp.where(dest == s, u, last[s]) for s in range(SLOTS))
        return last

    last = lax.fori_loop(0, PAIRS, walk, (jnp.int32(2 * PAIRS),) * SLOTS)
    for s in range(SLOTS):
        idx[4 * PAIRS + s] = last[s]

    share(0)

    scale = math.log2(math.e) / math.sqrt(DIM)

    def load(ref, u):
        return ref[dest_of(u)].reshape(HALF, DIM)

    def corner(t):
        kernel = jnp.exp2(dot(load(EA, 2 * t), load(EA, 2 * t + 1), NT) * scale)
        K[t, 0:HALF, 0:HALF] = kernel.astype(BF)
        S[2 * t + 1] = jnp.sum(kernel, axis=0, keepdims=True)
        S[2 * t] = jnp.sum((kernel[:, 0:128] + kernel[:, 128:256]).T, axis=0, keepdims=True)

    def rest(t):
        low_a, high_a = load(EA, 2 * t), load(EB, 2 * t)
        low_b, high_b = load(EA, 2 * t + 1), load(EB, 2 * t + 1)
        right = jnp.exp2(dot(jnp.concatenate([low_a, high_a], axis=0), high_b, NT) * scale)
        K[t, :, HALF:ROWS] = right.astype(BF)
        left = jnp.exp2(dot(high_a, low_b, NT) * scale)
        K[t, HALF:ROWS, 0:HALF] = left.astype(BF)
        part = right[:, 0:128] + right[:, 128:256]
        high_part = part[HALF:ROWS] + left[:, 0:128] + left[:, 128:256]
        low_rows = jnp.sum(part[0:HALF].T, axis=0, keepdims=True) + S[2 * t]
        high_rows = jnp.sum(high_part.T, axis=0, keepdims=True)
        low_cols = jnp.sum(left, axis=0, keepdims=True) + S[2 * t + 1]
        high_cols = jnp.sum(right, axis=0, keepdims=True)
        for u, low, high in ((2 * t, low_rows, high_rows), (2 * t + 1, low_cols, high_cols)):
            prev = prev_of(u)
            R[u, :, 0:HALF] = low + R[prev, :, 0:HALF]
            R[u, :, HALF:ROWS] = high + R[prev, :, HALF:ROWS]

    steps = PAIRS // UNROLL
    share_of_step = (SLOTS - 1) // steps

    @pl.loop(0, steps)
    def _(i):
        for j in range(share_of_step):
            forward(1, 1 + i * share_of_step + j)
        for j in range(UNROLL):
            corner(i * UNROLL + j)

    share(1)

    @pl.loop(0, steps)
    def _(i):
        for j in range(UNROLL):
            rest(i * UNROLL + j)

    def scale_labels(s):
        scaling = 1.0 / jnp.sqrt(R[last_of(s)])
        SC[s] = scaling
        O[s] = (L[s].astype(F32) * scaling).astype(BF)

    scale_labels(me)

    @pl.loop(1, SLOTS)
    def _(k):
        lab_copy(k).wait()
        scale_labels(source(k))

    def products(src, start, width):
        cols = slice(start, start + width)

        def pair(t):
            first, second = dest_of(2 * t), dest_of(2 * t + 1)
            to_first = dot(src[second], K[t, cols, :], NT)
            to_second = dot(src[first], K[t, :, cols], NN)
            for u, product in ((2 * t, to_first), (2 * t + 1, to_second)):
                T[u, :, 0:width] = product + T[prev_of(u), :, 0:width]

        @pl.loop(0, PAIRS // PAIR_UNROLL)
        def _(i):
            for j in range(PAIR_UNROLL):
                pair(i * PAIR_UNROLL + j)

    for h in range(2):
        cols = slice(h * HALF, (h + 1) * HALF)
        products(O, h * HALF, HALF)

        @pl.loop(0, SLOTS)
        def _(s):
            scaling = SC[s, :, cols]
            field = (ALPHA * scaling) * T[last_of(s)] + (1.0 - ALPHA) * L[s, :, cols].astype(F32)
            O2[s, :, cols] = (field * scaling).astype(BF)

    for h in range(CHUNKS):
        cols = slice(h * LANES, (h + 1) * LANES)
        products(O2, h * LANES, LANES)

        def finish(s):
            SB[s, :, cols] = ((ALPHA * SC[s, :, cols]) * T[last_of(s), :, 0:LANES]).astype(BF)

        @pl.loop(1, SLOTS)
        def _(k):
            finish(to(k))
            ret_copy(k, h).start()

        finish(me)
        ret_own(h).start()

    @pl.loop(1, SLOTS)
    def _(k):
        for p in range(2):
            for i in range(2):
                if p == 0 or i == 0:
                    emb_copy(p, k, i).wait_send()
                y_copy(p, k, i).wait_send()
            sib_copy(p, k).wait_send()
        pass_copy(k).wait_send()

    for h in range(CHUNKS):
        @pl.loop(1, SLOTS)
        def _(k):
            ret_copy(k, h).wait()

        ret_own(h).wait()
        cols = slice(h * LANES, (h + 1) * LANES)
        b = h % 2
        for s in range(SLOTS):
            W[b, pl.ds(s, PAD, stride=SLOTS), :] = LT[s * PAD : (s + 1) * PAD, cols].astype(F32)
        for i in range(SLOTS):
            O[i, :, cols] = W[b, i * PAD : (i + 1) * PAD, :].astype(BF)
        for copy in out_copies(h):
            copy.start()

    for h in range(CHUNKS):
        for copy in out_copies(h):
            copy.wait()


def body(embeddings, labels, block_pairs, block_slot):
    emb = embeddings.reshape(SLOTS, 2, SIDE, 2, HALF // (2 * SIDE), DIM)
    lab = jnp.transpose(labels, (1, 0, 2)).reshape(CLASSES * SLOTS, ROWS)
    sems = pltpu.SemaphoreType.DMA
    ret = pl.pallas_call(
        main_kernel,
        out_shape=jax.ShapeDtypeStruct((CLASSES * SLOTS, ROWS), BF),
        in_specs=[
            pl.BlockSpec(memory_space=pltpu.SMEM),
            pl.BlockSpec(memory_space=pltpu.SMEM),
            pl.BlockSpec(memory_space=pltpu.HBM),
            pl.BlockSpec(memory_space=pltpu.HBM),
        ],
        out_specs=pl.BlockSpec(memory_space=pl.ANY),
        scratch_shapes=[
            pltpu.VMEM((SLOTS, SIDE, 2, HALF // (2 * SIDE), DIM), BF),
            pltpu.VMEM((SLOTS, SIDE, 2, HALF // (2 * SIDE), DIM), BF),
            pltpu.VMEM((2 * PAIRS, 1, HALF), F32),
            pltpu.VMEM((PAIRS, ROWS, ROWS), BF),
            pltpu.VMEM((2 * PAIRS + 1, PAD, HALF), F32),
            pltpu.VMEM((2, SLOTS * PAD, LANES), F32),
            pltpu.VMEM((SLOTS * PAD, ROWS), BF),
            pltpu.VMEM((SLOTS, PAD, ROWS), BF),
            pltpu.VMEM((SLOTS, PAD, ROWS), BF),
            pltpu.VMEM((SLOTS, PAD, ROWS), BF),
            pltpu.VMEM((SLOTS, PAD, ROWS), BF),
            pltpu.VMEM((2 * PAIRS + 1, 1, ROWS), F32),
            pltpu.VMEM((SLOTS, 1, ROWS), F32),
            pltpu.SMEM((4 * PAIRS + SLOTS,), jnp.int32),
            sems((2, SLOTS, 2)), sems((2, SLOTS, 2)),
            sems((2, SLOTS, 2)), sems((2, SLOTS, 2)),
            sems((2, SLOTS)), sems((2, SLOTS)),
            sems((SLOTS,)), sems((SLOTS,)),
            sems((SLOTS,)), sems((SLOTS,)),
            sems((SLOTS, CHUNKS)), sems((SLOTS, CHUNKS)),
            sems((CHUNKS, SLOTS)),
            sems((CHUNKS,)),
        ],
        compiler_params=pltpu.CompilerParams(
            vmem_limit_bytes=58 * 2**20, collective_id=0, has_side_effects=True
        ),
    )(block_pairs.T, block_slot, emb, lab)
    out = ret.astype(F32) + (1.0 - ALPHA) * lab.astype(F32)
    return jnp.transpose(out.reshape(CLASSES, SLOTS, ROWS), (1, 0, 2))


def solution(mesh):
    return jax.shard_map(
        body,
        mesh=mesh,
        in_specs=(P("shard", None, None), P("shard", "rep", None), P(), P()),
        out_specs=P("shard", "rep", None),
        check_vma=False,
    )
```

```python
import functools
import math

import jax
import jax.numpy as jnp
from jax import lax
from jax.experimental import pallas as pl
from jax.experimental.pallas import tpu as pltpu
from jax.sharding import PartitionSpec as P

ITERS = 2
ALPHA = 0.9

SLOTS = 16
SIDE = 4
PAIRS = 40
ROWS = 512
DIM = 768
CLASSES = 125
PAD = 128
HALF = ROWS // 2
LANES = 128
UNROLL = 8
PAIR_UNROLL = 8
CHUNKS = ROWS // LANES

MESH = pl.DeviceIdType.MESH
NT = (((1,), (1,)), ((), ()))
NN = (((1,), (0,)), ((), ()))
BF = jnp.bfloat16
F32 = jnp.float32


def dot(a, b, dims):
    return lax.dot_general(a, b, dims, preferred_element_type=F32)


def main_kernel(
    pairs, slots, emb, lab, out,
    EA, EB, S, K, T, W, LT, SB, L, O, O2, R, SC, idx,
    se, re, sy, ry, sd, rd, sl, rl, sr, rr, so, loc,
):
    me = lax.axis_index("shard")
    rep = lax.axis_index("rep")
    y, core = rep // 2, rep % 2
    z, x = me // SIDE, me % SIDE
    up = ((y + 1) % SIDE) * 2 + core
    down = ((y + SIDE - 1) % SIDE) * 2 + core
    sibling = y * 2 + (1 - core)
    quarters = (y, (y + 2) % SIDE)

    def dest_of(u):
        return idx[u]

    def prev_of(u):
        return idx[2 * PAIRS + u]

    def last_of(s):
        return idx[4 * PAIRS + s]

    def offset(k):
        k = (k * 7) % SLOTS
        dz, dx = k // SIDE, k % SIDE
        return jnp.where(core == 0, dz, (SIDE - dx) % SIDE), jnp.where(core == 0, dx, (SIDE - dz) % SIDE)

    def to(k):
        dz, dx = offset(k)
        return ((z + dz) % SIDE) * SIDE + (x + dx) % SIDE

    def source(k):
        dz, dx = offset(k)
        return ((z + SIDE - dz) % SIDE) * SIDE + (x + SIDE - dx) % SIDE

    def remote(src, dst, send, recv, shard, r):
        return pltpu.make_async_remote_copy(
            src, dst, send, recv, device_id={"shard": shard, "rep": r}, device_id_type=MESH
        )

    def landing(g):
        return LT.at[pl.ds(g * PAD, PAD), :]

    halves = (EA, EB)

    def emb_copy(p, k, i):
        q = quarters[i]
        return remote(
            emb.at[to(k), p, q, core], halves[p].at[me, q, core], se.at[p, k, i], re.at[p, k, i], to(k), rep
        )

    def y_copy(p, k, i):
        piece = halves[p].at[source(k), y, core]
        return remote(piece, piece, sy.at[p, k, i], ry.at[p, k, i], me, (up, down)[i])

    def sib_copy(p, k):
        piece = halves[p].at[source(k), :, core]
        return remote(piece, piece, sd.at[p, k], rd.at[p, k], me, sibling)

    def own_emb(p):
        return pltpu.make_async_copy(emb.at[me, p], halves[p].at[me], loc.at[2 * p])

    def lab_copy(k):
        return remote(SB.at[to(k)], L.at[me], sl.at[k], rl.at[k], to(k), rep)

    def ret_copy(k, h):
        cols = pl.ds(h * LANES, LANES)
        return remote(
            SB.at[to(k), :, cols], landing(me).at[:, cols], sr.at[k, h], rr.at[k, h], to(k), rep
        )

    def ret_own(h):
        cols = pl.ds(h * LANES, LANES)
        return pltpu.make_async_copy(SB.at[me, :, cols], landing(me).at[:, cols], loc.at[h])

    def out_copies(h):
        cols = pl.ds(h * LANES, LANES)
        full = SLOTS * CLASSES // PAD
        rest = SLOTS * CLASSES - full * PAD
        yield from (
            pltpu.make_async_copy(O.at[i, :, cols], out.at[pl.ds(i * PAD, PAD), cols], so.at[h, i])
            for i in range(full)
        )
        yield pltpu.make_async_copy(
            O.at[full, pl.ds(0, rest), cols], out.at[pl.ds(full * PAD, rest), cols], so.at[h, full]
        )

    own_lab = pltpu.make_async_copy(lab, LT.at[pl.ds(0, SLOTS * CLASSES), :], loc.at[1])
    own_emb(0).start()
    own_emb(1).start()
    own_lab.start()

    barrier = pltpu.get_barrier_semaphore()

    @pl.loop(1, SLOTS)
    def _(k):
        pl.semaphore_signal(barrier, inc=1, device_id={"shard": to(k), "rep": rep}, device_id_type=MESH)

    for r in (up, down, sibling):
        pl.semaphore_signal(barrier, inc=1, device_id={"shard": me, "rep": r}, device_id_type=MESH)
    pl.semaphore_wait(barrier, SLOTS + 2)

    for p in range(2):
        for i in range(2):
            @pl.loop(1, SLOTS)
            def _(k):
                emb_copy(p, k, i).start()

    def forward(p, k):
        emb_copy(p, k, 0).wait_recv()
        y_copy(p, k, 0).start()
        y_copy(p, k, 1).start()

    def share(p):
        @pl.loop(1, SLOTS)
        def _(k):
            y_copy(p, k, 0).wait_recv()
            y_copy(p, k, 1).wait_recv()
            emb_copy(p, k, 1).wait_recv()
            sib_copy(p, k).start()

        @pl.loop(1, SLOTS)
        def _(k):
            sib_copy(p, k).wait_recv()

        own_emb(p).wait()

    T[2 * PAIRS] = jnp.zeros((PAD, HALF), F32)
    R[2 * PAIRS] = jnp.zeros((1, ROWS), F32)

    @pl.loop(1, SLOTS)
    def _(k):
        forward(0, k)

    own_lab.wait()
    for c in range(ROWS // LANES):
        cols = slice(c * LANES, (c + 1) * LANES)
        b = c % 2
        W[b, 0 : SLOTS * CLASSES, :] = LT[0 : SLOTS * CLASSES, cols].astype(F32)
        W[b, SLOTS * CLASSES : SLOTS * PAD, :] = jnp.zeros((SLOTS * (PAD - CLASSES), LANES), F32)
        for s in range(SLOTS):
            SB[s, :, cols] = W[b, pl.ds(s, PAD, stride=SLOTS), :].astype(BF)
    L[me] = SB[me]

    @pl.loop(1, SLOTS)
    def _(k):
        lab_copy(k).start()

    def walk(t, last):
        for end in range(2):
            u = 2 * t + end
            dest = slots[pairs[end, me * PAIRS + t]] // SLOTS
            idx[u] = dest
            prev = 2 * PAIRS
            for s in range(SLOTS):
                prev = jnp.where(dest == s, last[s], prev)
            idx[2 * PAIRS + u] = prev
            last = tuple(jnp.where(dest == s, u, last[s]) for s in range(SLOTS))
        return last

    last = lax.fori_loop(0, PAIRS, walk, (jnp.int32(2 * PAIRS),) * SLOTS)
    for s in range(SLOTS):
        idx[4 * PAIRS + s] = last[s]

    share(0)

    scale = math.log2(math.e) / math.sqrt(DIM)

    def load(ref, u):
        return ref[dest_of(u)].reshape(HALF, DIM)

    def corner(t):
        kernel = jnp.exp2(dot(load(EA, 2 * t), load(EA, 2 * t + 1), NT) * scale)
        K[t, 0:HALF, 0:HALF] = kernel.astype(BF)
        S[2 * t + 1] = jnp.sum(kernel, axis=0, keepdims=True)
        S[2 * t] = jnp.sum((kernel[:, 0:128] + kernel[:, 128:256]).T, axis=0, keepdims=True)

    def rest(t):
        low_a, high_a = load(EA, 2 * t), load(EB, 2 * t)
        low_b, high_b = load(EA, 2 * t + 1), load(EB, 2 * t + 1)
        right = jnp.exp2(dot(jnp.concatenate([low_a, high_a], axis=0), high_b, NT) * scale)
        K[t, :, HALF:ROWS] = right.astype(BF)
        left = jnp.exp2(dot(high_a, low_b, NT) * scale)
        K[t, HALF:ROWS, 0:HALF] = left.astype(BF)
        part = right[:, 0:128] + right[:, 128:256]
        high_part = part[HALF:ROWS] + left[:, 0:128] + left[:, 128:256]
        low_rows = jnp.sum(part[0:HALF].T, axis=0, keepdims=True) + S[2 * t]
        high_rows = jnp.sum(high_part.T, axis=0, keepdims=True)
        low_cols = jnp.sum(left, axis=0, keepdims=True) + S[2 * t + 1]
        high_cols = jnp.sum(right, axis=0, keepdims=True)
        for u, low, high in ((2 * t, low_rows, high_rows), (2 * t + 1, low_cols, high_cols)):
            prev = prev_of(u)
            R[u, :, 0:HALF] = low + R[prev, :, 0:HALF]
            R[u, :, HALF:ROWS] = high + R[prev, :, HALF:ROWS]

    steps = PAIRS // UNROLL
    share_of_step = (SLOTS - 1) // steps

    @pl.loop(0, steps)
    def _(i):
        for j in range(share_of_step):
            forward(1, 1 + i * share_of_step + j)
        for j in range(UNROLL):
            corner(i * UNROLL + j)

    share(1)

    @pl.loop(0, steps)
    def _(i):
        for j in range(UNROLL):
            rest(i * UNROLL + j)

    def scale_labels(s):
        scaling = 1.0 / jnp.sqrt(R[last_of(s)])
        SC[s] = scaling
        O[s] = (L[s].astype(F32) * scaling).astype(BF)

    scale_labels(me)

    @pl.loop(1, SLOTS)
    def _(k):
        lab_copy(k).wait()
        scale_labels(source(k))

    def products(src, start, width, unroll):
        cols = slice(start, start + width)

        def pair(t):
            first, second = dest_of(2 * t), dest_of(2 * t + 1)
            to_first = dot(src[second], K[t, cols, :], NT)
            to_second = dot(src[first], K[t, :, cols], NN)
            for u, product in ((2 * t, to_first), (2 * t + 1, to_second)):
                T[u, :, 0:width] = product + T[prev_of(u), :, 0:width]

        @pl.loop(0, PAIRS // unroll)
        def _(i):
            for j in range(unroll):
                pair(i * unroll + j)

    for h in range(2):
        cols = slice(h * HALF, (h + 1) * HALF)
        products(O, h * HALF, HALF, 20)

        @pl.loop(0, SLOTS)
        def _(s):
            scaling = SC[s, :, cols]
            field = (ALPHA * scaling) * T[last_of(s)] + (1.0 - ALPHA) * L[s, :, cols].astype(F32)
            O2[s, :, cols] = (field * scaling).astype(BF)

    for h in range(CHUNKS):
        cols = slice(h * LANES, (h + 1) * LANES)
        products(O2, h * LANES, LANES, PAIR_UNROLL)

        def finish(s):
            SB[s, :, cols] = ((ALPHA * SC[s, :, cols]) * T[last_of(s), :, 0:LANES]).astype(BF)

        @pl.loop(1, SLOTS)
        def _(k):
            finish(to(k))
            ret_copy(k, h).start()

        finish(me)
        ret_own(h).start()

    @pl.loop(1, SLOTS)
    def _(k):
        for p in range(2):
            for i in range(2):
                emb_copy(p, k, i).wait_send()
                y_copy(p, k, i).wait_send()
            sib_copy(p, k).wait_send()

    for h in range(CHUNKS):
        @pl.loop(1, SLOTS)
        def _(k):
            ret_copy(k, h).wait()

        ret_own(h).wait()
        cols = slice(h * LANES, (h + 1) * LANES)
        b = h % 2
        for s in range(SLOTS):
            W[b, pl.ds(s, PAD, stride=SLOTS), :] = LT[s * PAD : (s + 1) * PAD, cols].astype(F32)
        for i in range(SLOTS):
            O[i, :, cols] = W[b, i * PAD : (i + 1) * PAD, :].astype(BF)
        for copy in out_copies(h):
            copy.start()

    for h in range(CHUNKS):
        for copy in out_copies(h):
            copy.wait()


def body(embeddings, labels, block_pairs, block_slot):
    emb = embeddings.reshape(SLOTS, 2, SIDE, 2, HALF // (2 * SIDE), DIM)
    lab = jnp.transpose(labels, (1, 0, 2)).reshape(CLASSES * SLOTS, ROWS)
    sems = pltpu.SemaphoreType.DMA
    ret = pl.pallas_call(
        main_kernel,
        out_shape=jax.ShapeDtypeStruct((CLASSES * SLOTS, ROWS), BF),
        in_specs=[
            pl.BlockSpec(memory_space=pltpu.SMEM),
            pl.BlockSpec(memory_space=pltpu.SMEM),
            pl.BlockSpec(memory_space=pltpu.HBM),
            pl.BlockSpec(memory_space=pltpu.HBM),
        ],
        out_specs=pl.BlockSpec(memory_space=pl.ANY),
        scratch_shapes=[
            pltpu.VMEM((SLOTS, SIDE, 2, HALF // (2 * SIDE), DIM), BF),
            pltpu.VMEM((SLOTS, SIDE, 2, HALF // (2 * SIDE), DIM), BF),
            pltpu.VMEM((2 * PAIRS, 1, HALF), F32),
            pltpu.VMEM((PAIRS, ROWS, ROWS), BF),
            pltpu.VMEM((2 * PAIRS + 1, PAD, HALF), F32),
            pltpu.VMEM((2, SLOTS * PAD, LANES), F32),
            pltpu.VMEM((SLOTS * PAD, ROWS), BF),
            pltpu.VMEM((SLOTS, PAD, ROWS), BF),
            pltpu.VMEM((SLOTS, PAD, ROWS), BF),
            pltpu.VMEM((SLOTS, PAD, ROWS), BF),
            pltpu.VMEM((SLOTS, PAD, ROWS), BF),
            pltpu.VMEM((2 * PAIRS + 1, 1, ROWS), F32),
            pltpu.VMEM((SLOTS, 1, ROWS), F32),
            pltpu.SMEM((4 * PAIRS + SLOTS,), jnp.int32),
            sems((2, SLOTS, 2)), sems((2, SLOTS, 2)),
            sems((2, SLOTS, 2)), sems((2, SLOTS, 2)),
            sems((2, SLOTS)), sems((2, SLOTS)),
            sems((SLOTS,)), sems((SLOTS,)),
            sems((SLOTS, CHUNKS)), sems((SLOTS, CHUNKS)),
            sems((CHUNKS, SLOTS)),
            sems((CHUNKS,)),
        ],
        compiler_params=pltpu.CompilerParams(
            vmem_limit_bytes=58 * 2**20, collective_id=0, has_side_effects=True
        ),
    )(block_pairs.T, block_slot, emb, lab)
    out = ret.astype(F32) + (1.0 - ALPHA) * lab.astype(F32)
    return jnp.transpose(out.reshape(CLASSES, SLOTS, ROWS), (1, 0, 2))


def solution(mesh):
    return jax.shard_map(
        body,
        mesh=mesh,
        in_specs=(P("shard", None, None), P("shard", "rep", None), P(), P()),
        out_specs=P("shard", "rep", None),
        check_vma=False,
    )
```
